256 devices in a mesh: cluster: 16 (over z, core), group: 16 (over y, x).
Axes of the slice: x: 4, y: 4, z: 8, core: 2. Of those that a mesh axis runs over, the one named last changes fastest.
Arguments:
- loads: float32 [256, 8, 128, 256], P(('cluster', 'group')), parts along dimension 0, may hold values from -6 to 6
- multipliers: float32 [131072, 256], P(('cluster', 'group')), parts along dimension 0, may hold values from -6 to 6
- gluing: int32 [131072], P(('cluster', 'group')), parts along dimension 0, may hold values from 0 to 16383
- signs: int32 [131072], P(('cluster', 'group')), parts along dimension 0, may hold values 0 or 1
- parents: int32 [256, 7], P('cluster'), parts along dimension 0, may hold values from 0 to 15
- inverses: float32 [256, 8, 128, 128], P(('cluster', 'group')), parts along dimension 0
- to_parent: float32 [256, 7, 128, 128], P(('cluster', 'group')), parts along dimension 0, may hold values from -0.25 to 0.25
- grandparent_factor: float32 [256, 6, 128, 128], P(('cluster', 'group')), parts along dimension 0, may hold values from -0.25 to 0.25
Outputs:
- solved: float32 [256, 8, 128, 256], P(('cluster', 'group')), parts along dimension 0
The draws below stay inside these ranges and needn't reach their ends.
There are 16 independent parts, one for each index of `cluster`. The reference program is written for one: setup_inputs(seed, part) draws one part's arguments, and reference() takes and returns one part's arrays. A program takes and returns all parts, laid end to end along the dimension named above; each array names one. Nothing has to cross between parts.
Inputs may be any that keep to these rules, and one draw needn't show every extreme that they name: gluing[m] = (n * 8 + l) * 128 + i names row i of supernode n on level l; several multipliers may glue one unknown. parents[n, l] is the supernode on level l + 1 into which supernode n of level l is eliminated.
All inputs are finite; a program needn't handle non-finite values. No bound on the sum of `signs` on one device may be relied on, other than what follows from the above.
Results may differ from the reference program's by a relative error of at most 0.0001.
Values sent between devices are 32-bit elements; how exact they have to be, the bound alone decides.
A program may use at most 64 MiB of HBM per device.

```python
import jax
import jax.numpy as jnp
from jax import lax

B = 128
R = 256
LEV = 8
NPL = 16
DOFS = 16384
MULT = 8192


def draw_inverses(key, part):
    key = jax.random.fold_in(key, 11)
    noise = jax.random.normal(key, (NPL, LEV, B, B), jnp.float32) * (0.5 / B ** 0.5)
    rows_index = lax.broadcasted_iota(jnp.int32, (B, B), 0)
    cols_index = lax.broadcasted_iota(jnp.int32, (B, B), 1)
    identity = (rows_index == cols_index).astype(jnp.float32)
    return 0.8 * identity[None, None] + noise


def set_ends(result, rng, low, top_value):
    index_at = [jax.random.randint(jax.random.fold_in(rng, axis), (), 0, length) for axis, length in enumerate(result.shape)]
    main_axis = result.shape.index(max(result.shape))
    next_to = index_at[:main_axis] + [(index_at[main_axis] + 1) % result.shape[main_axis]] + index_at[main_axis + 1:]
    return result.at[tuple(index_at)].set(low).at[tuple(next_to)].set(top_value)


def block_scale(own_key, extent, shards, low, top_value):
    loudness = 1.0
    for position, shards_of in shards:
        steps = jax.random.uniform(jax.random.fold_in(jax.random.fold_in(own_key, 6), position), (shards_of,), jnp.float32, low / len(shards), top_value / len(shards))
        loudness = loudness * jnp.repeat(jnp.exp(steps), extent[position] // shards_of).reshape((-1,) + (1,) * (len(extent) - 1 - position))
    return loudness


def bell_draw(own_key, shape, scale, most, cuts=(), dtype=jnp.bfloat16):
    values = jax.random.normal(own_key, shape, jnp.float32) * scale
    if len(cuts) > 0:
        values = block_scale(own_key, shape, cuts, -0.22, 0.18) * values
    return jnp.clip(values, min=-most, max=most).astype(dtype)


def setup_inputs(seed: int = 0, part: int = 0) -> dict:
    seeds = jax.random.split(jax.random.key(seed), 9)
    part_splits = jax.random.split(jax.random.fold_in(seeds[8], part), 9)
    loads = bell_draw(part_splits[0], (NPL, LEV, B, R), 1.0, 6.0, ((0, 16),), jnp.float32)
    multipliers = bell_draw(part_splits[1], (MULT, R), 1.0, 6.0, ((0, 16),), jnp.float32)
    gluing = set_ends(jax.random.randint(part_splits[2], (MULT,), 0, DOFS), jax.random.fold_in(part_splits[2], 1), 0, DOFS - 1).astype(jnp.int32)
    signs = set_ends((jax.random.randint(part_splits[3], (MULT,), 0, 2) < 1).astype(jnp.int32), jax.random.fold_in(part_splits[3], 1), 0, 1)
    parents = set_ends(jax.random.randint(part_splits[4], (NPL, LEV - 1), 0, NPL), jax.random.fold_in(part_splits[4], 1), 0, NPL - 1).astype(jnp.int32)
    inverses = draw_inverses(jax.random.fold_in(jax.random.fold_in(seeds[8], part), 71), part)
    to_parent = bell_draw(part_splits[6], (NPL, LEV - 1, B, B), (4 * B) ** -0.5, 0.25, ((0, 16),), jnp.float32)
    grandparent_factor = bell_draw(part_splits[7], (NPL, LEV - 2, B, B), (4 * B) ** -0.5, 0.25, ((0, 16),), jnp.float32)
    return dict(loads=loads, multipliers=multipliers, gluing=gluing, signs=signs, parents=parents, inverses=inverses, to_parent=to_parent, grandparent_factor=grandparent_factor)


def reference(loads, multipliers, gluing, signs, parents, inverses, to_parent, grandparent_factor):
    coeff = (2 * signs - 1).astype(jnp.float32)
    glued = jnp.zeros((DOFS, R), jnp.float32).at[gluing].add(coeff[:, None] * multipliers)
    awaiting_contribution = loads - glued.reshape(NPL, LEV, B, R)
    solved = []
    for level in range(LEV):
        unknown_estimate = jnp.einsum("nij,njr->nir", inverses[:, level], awaiting_contribution[:, level], precision=lax.Precision.HIGHEST)
        solved.append(unknown_estimate)
        if level + 1 < LEV:
            first = parents[:, level]
            toward_root = jnp.einsum("nij,njr->nir", to_parent[:, level], unknown_estimate, precision=lax.Precision.HIGHEST)
            awaiting_contribution = awaiting_contribution.at[first, level + 1].add(-toward_root)
            if level + 2 < LEV:
                second_term = parents[first, level + 1]
                distant_ancestor = jnp.einsum("nij,njr->nir", grandparent_factor[:, level], unknown_estimate, precision=lax.Precision.HIGHEST)
                awaiting_contribution = awaiting_contribution.at[second_term, level + 2].add(-distant_ancestor)
    return jnp.stack(solved, axis=1)
```

```python
import jax
import jax.numpy as jnp
from jax import lax
from jax.experimental import pallas as pl
from jax.experimental.pallas import tpu as pltpu
from jax.sharding import PartitionSpec as P

CHUNKS = 4
SLOTS = 16
HEAD = 8


def split(x):
    high = x.astype(jnp.bfloat16)
    return high, (x - high.astype(jnp.float32)).astype(jnp.bfloat16)


def mm(a, b):
    return jnp.dot(a, b, preferred_element_type=jnp.float32)


def product(matrix, x):
    high, low = split(x)
    return mm(matrix[0], high) + (mm(matrix[0], low) + mm(matrix[1], high))


def kernel(
    loads, multipliers, gluing, signs, parents, inverses, to_parent, grandparent,
    out, flag,
    bucket, received, rows_high, rows_low, pending, parent_map,
    inv_h, inv_l, one_h, one_l, two_h, two_l,
    one_out, one_in, two_out, two_in, sum_out, sum_in, carried,
    pack_send, pack_recv, one_send, one_recv, two_send, two_recv, sum_send, sum_recv,
):
    nodes = parents.shape[0]
    levels, rows, columns = loads.shape[1:]
    count = multipliers.shape[0]
    me = lax.axis_index("group")
    others = nodes - 1

    def peer(k):
        return lax.rem(me + k, nodes)

    barrier = pltpu.get_barrier_semaphore()

    @pl.loop(1, nodes)
    def _(k):
        pl.semaphore_signal(barrier, inc=1, device_id={"group": peer(k)}, device_id_type=pl.DeviceIdType.MESH)

    dof = jnp.concatenate([gluing[i : i + 1, :] for i in range(gluing.shape[0])], axis=1)
    sign = jnp.concatenate([signs[i : i + 1, :] for i in range(signs.shape[0])], axis=1)
    coeff = (2 * sign - 1).astype(jnp.float32)
    span = levels * rows
    node = lax.div(dof, span)
    row = lax.rem(dof, span)
    order = lax.broadcasted_iota(jnp.int32, (1, count), 1)
    key = (dof * count + order).astype(jnp.float32)
    start = (node * (span * count)).astype(jnp.float32)
    rank = jnp.zeros((1, count), jnp.float32)
    for i in range(count // 128):
        lanes = jnp.broadcast_to(key[:, i * 128 : (i + 1) * 128], (128, 128))
        down = jnp.transpose(lanes)
        down = jnp.concatenate([down] * (count // 128), axis=1)
        before = (down < key) & (down >= start)
        rank = rank + jnp.sum(jnp.where(before, 1.0, 0.0), axis=0, keepdims=True)
    rank = rank.astype(jnp.int32)
    fits = rank < CHUNKS * SLOTS
    chunk = lax.div(rank, SLOTS)
    slot = lax.rem(rank, SLOTS)
    overflow = jnp.max(jnp.where(fits, 0.0, 1.0))

    place = jnp.where(fits, node * HEAD + chunk, -1)
    owner_rows = lax.broadcasted_iota(jnp.int32, (nodes * HEAD, count), 0) == place
    low_part = jnp.where(owner_rows, lax.rem(row, rows).astype(jnp.float32), 0.0).astype(jnp.bfloat16)
    high_part = jnp.where(owner_rows, (lax.div(row, rows) * rows).astype(jnp.float32), 0.0).astype(jnp.bfloat16)
    lane_of = lax.broadcasted_iota(jnp.int32, (nodes * SLOTS, count), 0) == SLOTS * me + slot
    lane_of = jnp.where(lane_of, 1.0, 0.0).astype(jnp.bfloat16)
    contract = (((1,), (1,)), ((), ()))
    header = lax.dot_general(low_part, lane_of, contract, preferred_element_type=jnp.float32)
    header = header + lax.dot_general(high_part, lane_of, contract, preferred_element_type=jnp.float32)
    last = lax.rem(lax.broadcasted_iota(jnp.int32, header.shape, 0), HEAD) == HEAD - 1
    header = jnp.where(last, overflow, header)
    bucket[:, 0:HEAD, :] = header.reshape(nodes, HEAD, columns)

    target = jnp.where(fits, chunk * (nodes * SLOTS) + node * SLOTS + slot, -1)
    m_high, m_low = split(multipliers[...])
    for j in range(CHUNKS):
        index = lax.broadcasted_iota(jnp.int32, (nodes * SLOTS, count), 0) + j * nodes * SLOTS
        table = jnp.where(index == target, coeff, 0.0).astype(jnp.bfloat16)
        packed = mm(table, m_high) + mm(table, m_low)
        first = HEAD + j * SLOTS
        bucket[:, first : first + SLOTS, :] = packed.reshape(nodes, SLOTS, columns)

    pl.semaphore_wait(barrier, others)

    def copy(source, target, send, recv, k):
        return pltpu.make_async_remote_copy(
            src_ref=source,
            dst_ref=target,
            send_sem=send,
            recv_sem=recv,
            device_id={"group": peer(k)},
            device_id_type=pl.DeviceIdType.MESH,
        )

    @pl.loop(1, nodes)
    def _(k):
        copy(bucket.at[peer(k)], received.at[me], pack_send.at[0], pack_recv.at[0], k).start()

    received[me] = bucket[me]

    @pl.loop(0, levels)
    def _(l):
        inv_h[l], inv_l[l] = split(inverses[0, l])

    @pl.loop(0, levels - 1)
    def _(l):
        one_h[l], one_l[l] = split(to_parent[0, l])

    @pl.loop(0, levels - 2)
    def _(l):
        two_h[l], two_l[l] = split(grandparent[0, l])

    chunk_rows = rows // nodes
    spread = lax.broadcasted_iota(jnp.int32, (nodes, rows), 1)
    spread = lax.div(spread, chunk_rows) == lax.broadcasted_iota(jnp.int32, (nodes, rows), 0)
    spread = jnp.where(spread, 1.0, 0.0).astype(jnp.bfloat16)
    across = lax.dot_general(
        parents[...].astype(jnp.float32).astype(jnp.bfloat16),
        spread,
        (((0,), (0,)), ((), ())),
        preferred_element_type=jnp.float32,
    )
    down_rows = lax.broadcasted_iota(jnp.int32, (rows, rows), 0)
    same = lax.rem(down_rows, chunk_rows) == lax.rem(
        lax.broadcasted_iota(jnp.int32, (rows, rows), 1), chunk_rows
    )
    down_node = lax.div(down_rows, chunk_rows)
    for l in range(levels - 1):
        hit = same & (down_node == across[l : l + 1, :].astype(jnp.int32))
        parent_map[l] = jnp.where(hit, 1.0, 0.0).astype(jnp.bfloat16)
    carried[...] = jnp.zeros_like(carried)
    sum_in[0] = jnp.zeros_like(sum_in[0])

    copy(bucket.at[pl.ds(0, others)], received.at[pl.ds(0, others)], pack_send.at[0], pack_recv.at[0], 1).wait_recv()

    head = received[0, 0:HEAD, :]
    for i in range(1, nodes):
        head = head + received[i, 0:HEAD, :]
    flag[...] = head[:, 0:128]
    width = nodes * SLOTS
    for j in range(CHUNKS):
        first = HEAD + j * SLOTS
        high, low = split(received[:, first : first + SLOTS, :].reshape(width, columns))
        rows_high[j * width : (j + 1) * width] = high
        rows_low[j * width : (j + 1) * width] = low
    wanted = jnp.concatenate([head[j : j + 1, :] for j in range(CHUNKS)], axis=1).astype(jnp.int32)

    @pl.loop(0, levels)
    def _(l):
        table = lax.broadcasted_iota(jnp.int32, (rows, CHUNKS * width), 0) + l * rows == wanted
        table = jnp.where(table, 1.0, 0.0).astype(jnp.bfloat16)
        pending[l] = loads[0, l] - (mm(table, rows_high[...]) + mm(table, rows_low[...]))

    def send(l, source, target, send_sem, recv_sem):
        @pl.loop(1, nodes)
        def _(k):
            copy(source.at[l, peer(k)], target.at[l, me], send_sem.at[l], recv_sem.at[l], k).start()

        target[l, me] = source[l, me]

    def arrived(l, source, target, send_sem, recv_sem):
        copy(
            source.at[l, pl.ds(0, others)], target.at[l, pl.ds(0, others)], send_sem.at[l], recv_sem.at[l], 1
        ).wait_recv()

    def sent(l, source, target, send_sem, recv_sem):
        copy(
            source.at[l, pl.ds(0, others)], target.at[l, pl.ds(0, others)], send_sem.at[l], recv_sem.at[l], 1
        ).wait_send()

    one = (one_out, one_in, one_send, one_recv)
    two = (two_out, two_in, two_send, two_recv)
    total = (sum_out, sum_in, sum_send, sum_recv)
    blocks = (nodes, chunk_rows, columns)

    def solve(l):
        x = pending[l] - sum_in[l].reshape(rows, columns)
        x = product((inv_h[l], inv_l[l]), x)
        out[0, l] = x
        return x

    @pl.loop(0, levels - 1)
    def _(l):
        x = solve(l)
        one_out[l] = product((one_h[l], one_l[l]), x).reshape(blocks)
        send(l, *one)

        @pl.when(l < levels - 2)
        def _():
            two_out[l] = product((two_h[l], two_l[l]), x).reshape(blocks)
            send(l, *two)

        arrived(l, *one)
        high, low = split(one_in[l].reshape(rows, columns) + carried[...])
        sum_out[l + 1] = (mm(parent_map[l], high) + mm(parent_map[l], low)).reshape(blocks)
        send(l + 1, *total)

        @pl.when(l < levels - 2)
        def _():
            arrived(l, *two)
            high, low = split(two_in[l].reshape(rows, columns))
            carried[...] = mm(parent_map[l], high) + mm(parent_map[l], low)

        arrived(l + 1, *total)

    solve(levels - 1)

    copy(bucket.at[pl.ds(0, others)], received.at[pl.ds(0, others)], pack_send.at[0], pack_recv.at[0], 1).wait_send()

    @pl.loop(0, levels - 1)
    def _(l):
        sent(l, *one)
        sent(l + 1, *total)

    @pl.loop(0, levels - 2)
    def _(l):
        sent(l, *two)


def direct(loads, multipliers, gluing, signs, parents, inverses, to_parent, grandparent_factor):
    nodes = parents.shape[0]
    _, levels, rows, columns = loads.shape
    count = multipliers.shape[0]
    f32, bf16 = jnp.float32, jnp.bfloat16
    room = HEAD + CHUNKS * SLOTS
    blocks = (nodes, rows // nodes, columns)
    square = (rows, rows)
    dma = pltpu.SemaphoreType.DMA
    vmem = pl.BlockSpec(memory_space=pltpu.VMEM)
    return pl.pallas_call(
        kernel,
        out_shape=(
            jax.ShapeDtypeStruct(loads.shape, f32),
            jax.ShapeDtypeStruct((HEAD, 128), f32),
        ),
        in_specs=[vmem] * 8,
        out_specs=(vmem, vmem),
        scratch_shapes=[
            pltpu.VMEM((nodes, room, columns), f32),
            pltpu.VMEM((nodes, room, columns), f32),
            pltpu.VMEM((nodes * CHUNKS * SLOTS, columns), bf16),
            pltpu.VMEM((nodes * CHUNKS * SLOTS, columns), bf16),
            pltpu.VMEM((levels, rows, columns), f32),
            pltpu.VMEM((levels - 1, *square), bf16),
            pltpu.VMEM((levels, *square), bf16),
            pltpu.VMEM((levels, *square), bf16),
            pltpu.VMEM((levels - 1, *square), bf16),
            pltpu.VMEM((levels - 1, *square), bf16),
            pltpu.VMEM((levels - 2, *square), bf16),
            pltpu.VMEM((levels - 2, *square), bf16),
            pltpu.VMEM((levels - 1, *blocks), f32),
            pltpu.VMEM((levels - 1, *blocks), f32),
            pltpu.VMEM((levels - 2, *blocks), f32),
            pltpu.VMEM((levels - 2, *blocks), f32),
            pltpu.VMEM((levels, *blocks), f32),
            pltpu.VMEM((levels, *blocks), f32),
            pltpu.VMEM((rows, columns), f32),
            dma((1,)),
            dma((1,)),
            dma((levels - 1,)),
            dma((levels - 1,)),
            dma((levels - 2,)),
            dma((levels - 2,)),
            dma((levels,)),
            dma((levels,)),
        ],
        compiler_params=pltpu.CompilerParams(
            collective_id=0, has_side_effects=True, vmem_limit_bytes=48 * 1024 * 1024
        ),
    )(
        loads,
        multipliers,
        gluing.reshape(count // 128, 128),
        signs.reshape(count // 128, 128),
        parents,
        inverses,
        to_parent,
        grandparent_factor,
    )


def general(loads, multipliers, gluing, signs, parents, inverses, to_parent, grandparent_factor):
    me = lax.axis_index("group")
    tree_depths = loads.shape[1]
    rows = loads.shape[2]
    span = tree_depths * rows
    coeff = (2 * signs - 1).astype(jnp.float32)
    target = lax.iota(jnp.int32, lax.axis_size("group") * span)
    table = jnp.where(target[:, None] == gluing[None, :], coeff[None, :], 0.0)
    glued = lax.psum_scatter(
        jnp.dot(
            table, multipliers, precision=lax.Precision.HIGHEST, preferred_element_type=jnp.float32
        ),
        "group",
        scatter_dimension=0,
        tiled=True,
    )
    awaiting_contribution = [
        loads[0, level] - glued[level * rows : (level + 1) * rows] for level in range(tree_depths)
    ]
    node_count = parents.shape[0]
    solved = []
    for level in range(tree_depths):
        unknown_estimate = jnp.dot(
            inverses[0, level],
            awaiting_contribution[level],
            precision=lax.Precision.HIGHEST,
            preferred_element_type=jnp.float32,
        )
        solved.append(unknown_estimate)
        if level + 1 < tree_depths:
            first = parents[:, level]
            if level + 2 < tree_depths:
                match = first[:, None] == lax.iota(jnp.int32, node_count)[None, :]
                second_term = jnp.sum(jnp.where(match, parents[None, :, level + 1], 0), axis=1)
                targets = jnp.stack([first, second_term], axis=1)
                panel_sequence = jnp.stack([to_parent[0, level], grandparent_factor[0, level]])
            else:
                targets = first[:, None]
                panel_sequence = to_parent[0, level][None]
            update_terms = jnp.einsum(
                "xdf,fh->xdh", panel_sequence, unknown_estimate, precision=lax.Precision.HIGHEST
            )[None]
            weight = (targets == me).astype(jnp.float32)
            moved = jnp.einsum(
                "km,kmbr->mbr",
                weight,
                lax.all_gather(update_terms, "group", axis=0, tiled=True),
                precision=lax.Precision.HIGHEST,
            )
            awaiting_contribution[level + 1] = awaiting_contribution[level + 1] - moved[0]
            if level + 2 < tree_depths:
                awaiting_contribution[level + 2] = awaiting_contribution[level + 2] - moved[1]
    return jnp.stack(solved)[None]


def body(*args):
    solved, flag = direct(*args)
    return lax.cond(flag[HEAD - 1, 0] > 0, lambda: general(*args), lambda: solved)


def solution(mesh):
    return jax.shard_map(
        body,
        mesh=mesh,
        in_specs=(
            P(("cluster", "group"), None, None, None),
            P(("cluster", "group"), None),
            P(("cluster", "group")),
            P(("cluster", "group")),
            P("cluster", None),
            P(("cluster", "group"), None, None, None),
            P(("cluster", "group"), None, None, None),
            P(("cluster", "group"), None, None, None),
        ),
        out_specs=P(("cluster", "group"), None, None, None),
        check_vma=False,
    )
```

```python
import jax
import jax.numpy as jnp
from jax import lax
from jax.experimental import pallas as pl
from jax.experimental.pallas import tpu as pltpu
from jax.sharding import PartitionSpec as P

CHUNKS = 4
SLOTS = 16
HEAD = 8


def split(x):
    high = x.astype(jnp.bfloat16)
    return high, (x - high.astype(jnp.float32)).astype(jnp.bfloat16)


def mm(a, b):
    return jnp.dot(a, b, preferred_element_type=jnp.float32)


def product(matrix, x):
    high, low = split(x)
    return mm(matrix[0], high) + (mm(matrix[0], low) + mm(matrix[1], high))


def kernel(
    loads, multipliers, gluing, signs, parents, inverses, to_parent, grandparent,
    out, flag,
    bucket, received, rows_high, rows_low, pending, parent_map, child_map, near_map, far_map,
    inv_h, inv_l, near_h, near_l, far_h, far_l, six_h, six_l, step_five,
    up_out, up_in, down_out, down_in, item_out, item_in, root_out, root_in,
    pack_send, pack_recv, up_send, up_recv, down_send, down_recv, item_send, item_recv, root_send, root_recv,
):
    nodes = parents.shape[0]
    levels, rows, columns = loads.shape[1:]
    count = multipliers.shape[0]
    me = lax.axis_index("group")
    others = nodes - 1
    part = rows // nodes
    rounds = levels // 2 - 1
    blocks = (nodes, part, columns)

    def peer(k):
        def shift(t):
            return jnp.where(t < 2, t + 2, 3 - t)

        y = lax.rem(lax.div(me, 4) + shift(lax.div(k, 4)), 4)
        x = lax.rem(lax.rem(me, 4) + shift(lax.rem(k, 4)), 4)
        return 4 * y + x

    def copy(source, target, send, recv, device):
        return pltpu.make_async_remote_copy(
            src_ref=source,
            dst_ref=target,
            send_sem=send,
            recv_sem=recv,
            device_id={"group": device},
            device_id_type=pl.DeviceIdType.MESH,
        )

    class Exchange:
        def __init__(self, source, target, send, recv):
            self.source, self.target, self.send, self.recv = source, target, send, recv

        def start(self):
            @pl.loop(0, others)
            def _(k):
                device = peer(k)
                copy(self.source.at[device], self.target.at[me], self.send, self.recv, device).start()

            self.target[me] = self.source[me]

        def all(self):
            most = pl.ds(0, others)
            return copy(self.source.at[most], self.target.at[most], self.send, self.recv, peer(0))

        def arrived(self):
            self.all().wait_recv()

        def sent(self):
            self.all().wait_send()

    def item(i):
        return Exchange(item_out.at[i], item_in.at[i], item_send.at[i], item_recv.at[i])

    pack = Exchange(bucket, received, pack_send.at[0], pack_recv.at[0])
    up = [Exchange(up_out.at[r], up_in.at[r], up_send.at[r], up_recv.at[r]) for r in range(rounds)]
    down = [Exchange(down_out.at[r], down_in.at[r], down_send.at[r], down_recv.at[r]) for r in range(rounds)]
    step_up = [item(r) for r in range(rounds)]
    step_down = [item(rounds + r) for r in range(rounds)]
    ask_up = [item(2 * rounds + r) for r in range(rounds)]
    ask_down = [item(3 * rounds + r) for r in range(rounds)]
    tail_up = item(4 * rounds)
    root_down = item(4 * rounds + 1)
    root_up = Exchange(root_out, root_in, root_send.at[0], root_recv.at[0])
    everything = [pack, *up, *down, *step_up, *step_down, *ask_up, *ask_down, tail_up, root_down, root_up]

    barrier = pltpu.get_barrier_semaphore()

    @pl.loop(0, others)
    def _(k):
        pl.semaphore_signal(barrier, inc=1, device_id={"group": peer(k)}, device_id_type=pl.DeviceIdType.MESH)

    def pair(level):
        both = jnp.concatenate([to_parent[0, level], grandparent[0, level]], axis=0)
        return product(split(both), inverses[0, level])

    def ask(r, both):
        near_h[r], near_l[r] = split(both)
        item_out[2 * rounds + r] = jnp.concatenate([both[:rows], both[rows:]], axis=1).reshape(blocks)

    ask(0, pair(1))

    spread = lax.div(lax.broadcasted_iota(jnp.int32, (nodes, rows), 1), part)
    spread = spread == lax.broadcasted_iota(jnp.int32, (nodes, rows), 0)
    spread = jnp.where(spread, 1.0, 0.0).astype(jnp.bfloat16)
    names = parents[...].astype(jnp.float32).astype(jnp.bfloat16)
    over = (((0,), (0,)), ((), ()))
    across = lax.dot_general(names, spread, over, preferred_element_type=jnp.float32).astype(jnp.int32)
    along = lax.dot_general(spread, names, over, preferred_element_type=jnp.float32).astype(jnp.int32)
    place_r = lax.broadcasted_iota(jnp.int32, (rows, rows), 0)
    place_c = lax.broadcasted_iota(jnp.int32, (rows, rows), 1)
    same = lax.rem(place_r, part) == lax.rem(place_c, part)
    for l in range(levels - 1):
        hit = same & (lax.div(place_r, part) == across[l : l + 1, :])
        parent_map[l] = jnp.where(hit, 1.0, 0.0).astype(jnp.bfloat16)
        hit = same & (lax.div(place_c, part) == along[:, l : l + 1])
        child_map[l] = jnp.where(hit, 1.0, 0.0).astype(jnp.bfloat16)

    pl.semaphore_wait(barrier, others)
    ask_up[0].start()

    dof = jnp.concatenate([gluing[i : i + 1, :] for i in range(gluing.shape[0])], axis=1)
    sign = jnp.concatenate([signs[i : i + 1, :] for i in range(signs.shape[0])], axis=1)
    coeff = (2 * sign - 1).astype(jnp.float32)
    span = levels * rows
    node = lax.div(dof, span)
    row = lax.rem(dof, span)
    order = lax.broadcasted_iota(jnp.int32, (1, count), 1)
    key = (dof * count + order).astype(jnp.float32)
    first_key = (node * (span * count)).astype(jnp.float32)
    rank = jnp.zeros((1, count), jnp.float32)
    for i in range(count // 128):
        lanes = jnp.broadcast_to(key[:, i * 128 : (i + 1) * 128], (128, 128))
        down_key = jnp.transpose(lanes)
        down_key = jnp.concatenate([down_key] * (count // 128), axis=1)
        before = (down_key < key) & (down_key >= first_key)
        rank = rank + jnp.sum(jnp.where(before, 1.0, 0.0), axis=0, keepdims=True)
    rank = rank.astype(jnp.int32)
    fits = rank < CHUNKS * SLOTS
    chunk = lax.div(rank, SLOTS)
    slot = lax.rem(rank, SLOTS)
    overflow = jnp.max(jnp.where(fits, 0.0, 1.0))

    place = jnp.where(fits, node * HEAD + chunk, -1)
    owner_rows = lax.broadcasted_iota(jnp.int32, (nodes * HEAD, count), 0) == place
    low_part = jnp.where(owner_rows, lax.rem(row, rows).astype(jnp.float32), 0.0).astype(jnp.bfloat16)
    high_part = jnp.where(owner_rows, (lax.div(row, rows) * rows).astype(jnp.float32), 0.0).astype(jnp.bfloat16)
    lane_of = lax.broadcasted_iota(jnp.int32, (nodes * SLOTS, count), 0) == SLOTS * me + slot
    lane_of = jnp.where(lane_of, 1.0, 0.0).astype(jnp.bfloat16)
    contract = (((1,), (1,)), ((), ()))
    header = lax.dot_general(low_part, lane_of, contract, preferred_element_type=jnp.float32)
    header = header + lax.dot_general(high_part, lane_of, contract, preferred_element_type=jnp.float32)
    last = lax.rem(lax.broadcasted_iota(jnp.int32, header.shape, 0), HEAD) == HEAD - 1
    header = jnp.where(last, overflow, header)
    bucket[:, 0:HEAD, :] = header.reshape(nodes, HEAD, columns)

    target = jnp.where(fits, chunk * (nodes * SLOTS) + node * SLOTS + slot, -1)
    m_high, m_low = split(multipliers[...])
    for j in range(CHUNKS):
        index = lax.broadcasted_iota(jnp.int32, (nodes * SLOTS, count), 0) + j * nodes * SLOTS
        table = jnp.where(index == target, coeff, 0.0).astype(jnp.bfloat16)
        packed = mm(table, m_high) + mm(table, m_low)
        first = HEAD + j * SLOTS
        bucket[:, first : first + SLOTS, :] = packed.reshape(nodes, SLOTS, columns)
    pack.start()

    ask(1, pair(3))
    ask_up[1].start()
    six = product(split(to_parent[0, levels - 2]), inverses[0, levels - 2])
    six_h[...], six_l[...] = split(six)
    root_out[...] = six.reshape(nodes, part, rows)
    root_up.start()
    step_five[...] = pair(5)

    @pl.loop(0, levels)
    def _(l):
        inv_h[l], inv_l[l] = split(inverses[0, l])

    def chain(a, b):
        return mm(a, b).astype(jnp.bfloat16)

    for r in range(rounds):
        w0, w1, w2 = parent_map[2 * r], parent_map[2 * r + 1], parent_map[2 * r + 2]
        near_map[r] = jnp.concatenate([w1, chain(w1, w0)], axis=1)
        both = chain(w2, w1)
        far_map[r] = jnp.concatenate([both, chain(both, w0), w2], axis=1)

    def gather(table, values):
        high, low = split(values)
        return mm(table, high) + mm(table, low)

    def answer(r):
        ask_up[r].arrived()
        found = gather(child_map[2 * r], item_in[2 * rounds + r].reshape(rows, columns))
        item_out[3 * rounds + r] = found.reshape(blocks)
        ask_down[r].start()

    def compose(r):
        ask_down[r].arrived()
        found = item_in[3 * rounds + r].reshape(rows, columns)
        found = jnp.concatenate([found[:, :rows], found[:, rows:]], axis=0)
        step = to_parent[0, 2 * r]
        leap = grandparent[0, 2 * r]
        made = product(split(found), step)
        far = -made[rows:]
        if r == rounds - 1:
            beyond = item_in[4 * rounds + 1].reshape(rows, columns)[:, rows:]
            far = far - product(split(beyond), leap)
        whole = jnp.concatenate([leap - made[:rows], far, step], axis=0)
        far_h[r], far_l[r] = split(whole)

    answer(0)
    pack.arrived()
    head = received[0, 0:HEAD, :]
    for i in range(1, nodes):
        head = head + received[i, 0:HEAD, :]
    flag[...] = head[:, 0:128]
    width = nodes * SLOTS
    for j in range(CHUNKS):
        first = HEAD + j * SLOTS
        high, low = split(received[:, first : first + SLOTS, :].reshape(width, columns))
        rows_high[j * width : (j + 1) * width] = high
        rows_low[j * width : (j + 1) * width] = low
    wanted = jnp.concatenate([head[j : j + 1, :] for j in range(CHUNKS)], axis=1).astype(jnp.int32)

    @pl.loop(0, levels)
    def _(l):
        table = lax.broadcasted_iota(jnp.int32, (rows, CHUNKS * width), 0) + l * rows == wanted
        table = jnp.where(table, 1.0, 0.0).astype(jnp.bfloat16)
        pending[l] = loads[0, l] - (mm(table, rows_high[...]) + mm(table, rows_low[...]))

    compose(0)

    def solve(level, x):
        x = product((inv_h[level], inv_l[level]), x)
        out[0, level] = x
        return x

    def skipped(r):
        step_down[r].arrived()
        solve(2 * r + 1, pending[2 * r + 1] - item_in[rounds + r].reshape(rows, columns))

    for r in range(rounds):
        level = 2 * r
        if r > 0:
            pending[level] = pending[level] - down_in[r - 1, :, :part].reshape(rows, columns)
            pending[level + 1] = pending[level + 1] - down_in[r - 1, :, part:].reshape(rows, columns)
        e = product((near_h[r], near_l[r]), pending[level + 1])
        up_out[r, :, 0:part] = e[:rows].reshape(blocks)
        up_out[r, :, 2 * part : 3 * part] = e[rows:].reshape(blocks)
        x = solve(level, pending[level])
        c = product((far_h[r, : 2 * rows], far_l[r, : 2 * rows]), x)
        up_out[r, :, part : 2 * part] = c[:rows].reshape(blocks)
        up_out[r, :, 3 * part :] = c[rows:].reshape(blocks)
        up[r].start()
        item_out[r] = product((far_h[r, 2 * rows :], far_l[r, 2 * rows :]), x).reshape(blocks)
        step_up[r].start()

        if r == 0:
            answer(1)
            root_up.arrived()
            six_in = root_in[...].reshape(rows, rows)
            above = gather(child_map[5], six_in)
            above = jnp.concatenate([above, gather(child_map[4], above)], axis=1)
            item_out[4 * rounds + 1] = above.reshape(blocks)
            root_down.start()
            item_out[4 * rounds] = product((six_h[...], six_l[...]), pending[levels - 2]).reshape(blocks)
            tail_up.start()
        else:
            skipped(r - 1)
        if r == 1:
            answer(2)

        up[r].arrived()
        first = jnp.concatenate([up_in[r, :, i * part : (i + 1) * part].reshape(rows, columns) for i in (0, 1)], axis=0)
        down_out[r, :, :part] = gather(near_map[r], first).reshape(blocks)
        second = jnp.concatenate([up_in[r, :, i * part : (i + 1) * part].reshape(rows, columns) for i in (2, 3)], axis=0)
        if r == rounds - 1:
            tail_up.arrived()
            second = jnp.concatenate([second, item_in[4 * rounds].reshape(rows, columns)], axis=0)
            second = gather(far_map[r], second)
        else:
            second = gather(far_map[r, :, : 2 * rows], second)
        down_out[r, :, part:] = second.reshape(blocks)
        down[r].start()
        step_up[r].arrived()
        item_out[rounds + r] = gather(parent_map[level], item_in[r].reshape(rows, columns)).reshape(blocks)
        step_down[r].start()

        if r == 0:
            root_down.arrived()
            beyond = item_in[4 * rounds + 1].reshape(rows, columns)[:, :rows]
            five = step_five[...]
            ask(2, jnp.concatenate([five[:rows], five[rows:] - product(split(beyond), five[:rows])], axis=0))
            ask_up[2].start()
        if r < rounds - 1:
            compose(r + 1)
        down[r].arrived()

    solve(levels - 2, pending[levels - 2] - down_in[rounds - 1, :, :part].reshape(rows, columns))
    solve(levels - 1, pending[levels - 1] - down_in[rounds - 1, :, part:].reshape(rows, columns))
    skipped(rounds - 1)

    for exchange in everything:
        exchange.sent()


def direct(loads, multipliers, gluing, signs, parents, inverses, to_parent, grandparent_factor):
    nodes = parents.shape[0]
    _, levels, rows, columns = loads.shape
    count = multipliers.shape[0]
    f32, bf16 = jnp.float32, jnp.bfloat16
    room = HEAD + CHUNKS * SLOTS
    rounds = levels // 2 - 1
    part = rows // nodes
    items = 4 * rounds + 2
    dma = pltpu.SemaphoreType.DMA
    vmem = pl.BlockSpec(memory_space=pltpu.VMEM)
    return pl.pallas_call(
        kernel,
        out_shape=(
            jax.ShapeDtypeStruct(loads.shape, f32),
            jax.ShapeDtypeStruct((HEAD, 128), f32),
        ),
        in_specs=[vmem] * 8,
        out_specs=(vmem, vmem),
        scratch_shapes=[
            pltpu.VMEM((nodes, room, columns), f32),
            pltpu.VMEM((nodes, room, columns), f32),
            pltpu.VMEM((nodes * CHUNKS * SLOTS, columns), bf16),
            pltpu.VMEM((nodes * CHUNKS * SLOTS, columns), bf16),
            pltpu.VMEM((levels, rows, columns), f32),
            pltpu.VMEM((levels - 1, rows, rows), bf16),
            pltpu.VMEM((levels - 1, rows, rows), bf16),
            pltpu.VMEM((rounds, rows, 2 * rows), bf16),
            pltpu.VMEM((rounds, rows, 3 * rows), bf16),
            pltpu.VMEM((levels, rows, rows), bf16),
            pltpu.VMEM((levels, rows, rows), bf16),
            pltpu.VMEM((rounds, 2 * rows, rows), bf16),
            pltpu.VMEM((rounds, 2 * rows, rows), bf16),
            pltpu.VMEM((rounds, 3 * rows, rows), bf16),
            pltpu.VMEM((rounds, 3 * rows, rows), bf16),
            pltpu.VMEM((rows, rows), bf16),
            pltpu.VMEM((rows, rows), bf16),
            pltpu.VMEM((2 * rows, rows), f32),
            pltpu.VMEM((rounds, nodes, 4 * part, columns), f32),
            pltpu.VMEM((rounds, nodes, 4 * part, columns), f32),
            pltpu.VMEM((rounds, nodes, 2 * part, columns), f32),
            pltpu.VMEM((rounds, nodes, 2 * part, columns), f32),
            pltpu.VMEM((items, nodes, part, columns), f32),
            pltpu.VMEM((items, nodes, part, columns), f32),
            pltpu.VMEM((nodes, part, rows), f32),
            pltpu.VMEM((nodes, part, rows), f32),
            dma((1,)),
            dma((1,)),
            dma((rounds,)),
            dma((rounds,)),
            dma((rounds,)),
            dma((rounds,)),
            dma((items,)),
            dma((items,)),
            dma((1,)),
            dma((1,)),
        ],
        compiler_params=pltpu.CompilerParams(
            collective_id=0, has_side_effects=True, vmem_limit_bytes=48 * 1024 * 1024
        ),
    )(
        loads,
        multipliers,
        gluing.reshape(count // 128, 128),
        signs.reshape(count // 128, 128),
        parents,
        inverses,
        to_parent,
        grandparent_factor,
    )


def general(loads, multipliers, gluing, signs, parents, inverses, to_parent, grandparent_factor):
    me = lax.axis_index("group")
    tree_depths = loads.shape[1]
    rows = loads.shape[2]
    span = tree_depths * rows
    coeff = (2 * signs - 1).astype(jnp.float32)
    target = lax.iota(jnp.int32, lax.axis_size("group") * span)
    table = jnp.where(target[:, None] == gluing[None, :], coeff[None, :], 0.0)
    glued = lax.psum_scatter(
        jnp.dot(
            table, multipliers, precision=lax.Precision.HIGHEST, preferred_element_type=jnp.float32
        ),
        "group",
        scatter_dimension=0,
        tiled=True,
    )
    awaiting_contribution = [
        loads[0, level] - glued[level * rows : (level + 1) * rows] for level in range(tree_depths)
    ]
    node_count = parents.shape[0]
    solved = []
    for level in range(tree_depths):
        unknown_estimate = jnp.dot(
            inverses[0, level],
            awaiting_contribution[level],
            precision=lax.Precision.HIGHEST,
            preferred_element_type=jnp.float32,
        )
        solved.append(unknown_estimate)
        if level + 1 < tree_depths:
            first = parents[:, level]
            if level + 2 < tree_depths:
                match = first[:, None] == lax.iota(jnp.int32, node_count)[None, :]
                second_term = jnp.sum(jnp.where(match, parents[None, :, level + 1], 0), axis=1)
                targets = jnp.stack([first, second_term], axis=1)
                panel_sequence = jnp.stack([to_parent[0, level], grandparent_factor[0, level]])
            else:
                targets = first[:, None]
                panel_sequence = to_parent[0, level][None]
            update_terms = jnp.einsum(
                "xdf,fh->xdh", panel_sequence, unknown_estimate, precision=lax.Precision.HIGHEST
            )[None]
            weight = (targets == me).astype(jnp.float32)
            moved = jnp.einsum(
                "km,kmbr->mbr",
                weight,
                lax.all_gather(update_terms, "group", axis=0, tiled=True),
                precision=lax.Precision.HIGHEST,
            )
            awaiting_contribution[level + 1] = awaiting_contribution[level + 1] - moved[0]
            if level + 2 < tree_depths:
                awaiting_contribution[level + 2] = awaiting_contribution[level + 2] - moved[1]
    return jnp.stack(solved)[None]


def body(*args):
    solved, flag = direct(*args)
    return lax.cond(flag[HEAD - 1, 0] > 0, lambda: general(*args), lambda: solved)


def solution(mesh):
    return jax.shard_map(
        body,
        mesh=mesh,
        in_specs=(
            P(("cluster", "group"), None, None, None),
            P(("cluster", "group"), None),
            P(("cluster", "group")),
            P(("cluster", "group")),
            P("cluster", None),
            P(("cluster", "group"), None, None, None),
            P(("cluster", "group"), None, None, None),
            P(("cluster", "group"), None, None, None),
        ),
        out_specs=P(("cluster", "group"), None, None, None),
        check_vma=False,
    )
```

```python
import jax
import jax.numpy as jnp
from jax import lax
from jax.experimental import pallas as pl
from jax.experimental.pallas import tpu as pltpu
from jax.sharding import PartitionSpec as P

CHUNKS = 4
SLOTS = 16
HEAD = 8
EARLY = 2


def split(x):
    high = x.astype(jnp.bfloat16)
    return high, (x - high.astype(jnp.float32)).astype(jnp.bfloat16)


def mm(a, b):
    return jnp.dot(a, b, preferred_element_type=jnp.float32)


def halves(matrix):
    return jnp.concatenate(split(matrix), axis=1)


def product(matrix, x):
    high, low = split(x)
    return mm(matrix, jnp.concatenate([high, high], axis=0)) + mm(matrix[:, : matrix.shape[1] // 2], low)


def kernel(
    loads_hbm, multipliers_hbm, gluing_hbm, signs_hbm, parents_hbm, inverses_hbm, to_parent_hbm, grandparent_hbm,
    out, flag,
    loads, multipliers, gluing, signs, parents, inverses, to_parent, grandparent, fetched,
    bucket, received, late_bucket, late_received, rows_high, rows_low, pending, parent_map, child_map, near_map, far_map,
    inverse, near, far, six, step_five,
    up_out, up_in, down_out, down_in, item_out, item_in, root_out, root_in,
    pack_send, pack_recv, up_send, up_recv, down_send, down_recv, item_send, item_recv, root_send, root_recv,
):
    nodes = parents.shape[1]
    levels, rows, columns = loads.shape[1:]
    count = multipliers.shape[0]
    me = lax.axis_index("group")
    others = nodes - 1
    part = rows // nodes
    rounds = levels // 2 - 1
    blocks = (nodes, part, columns)

    arguments = (
        (parents_hbm, parents),
        (to_parent_hbm, to_parent),
        (grandparent_hbm, grandparent),
        (inverses_hbm, inverses),
        (gluing_hbm, gluing),
        (signs_hbm, signs),
        (multipliers_hbm, multipliers),
        (loads_hbm, loads),
    )
    fetches = [pltpu.make_async_copy(far, near, fetched.at[i]) for i, (far, near) in enumerate(arguments)]
    for fetch in fetches:
        fetch.start()

    def peer(k):
        def shift(t):
            return jnp.where(t < 2, t + 2, 3 - t)

        y = lax.rem(lax.div(me, 4) + shift(lax.div(k, 4)), 4)
        x = lax.rem(lax.rem(me, 4) + shift(lax.rem(k, 4)), 4)
        return 4 * y + x

    def copy(source, target, send, recv, device):
        return pltpu.make_async_remote_copy(
            src_ref=source,
            dst_ref=target,
            send_sem=send,
            recv_sem=recv,
            device_id={"group": device},
            device_id_type=pl.DeviceIdType.MESH,
        )

    class Exchange:
        def __init__(self, source, target, send, recv):
            self.source, self.target, self.send, self.recv = source, target, send, recv

        def start(self):
            @pl.loop(0, others)
            def _(k):
                device = peer(k)
                copy(self.source.at[device], self.target.at[me], self.send, self.recv, device).start()

            self.target[me] = self.source[me]

        def all(self):
            most = pl.ds(0, others)
            return copy(self.source.at[most], self.target.at[most], self.send, self.recv, peer(0))

        def arrived(self):
            self.all().wait_recv()

        def sent(self):
            self.all().wait_send()

    def item(i):
        return Exchange(item_out.at[i], item_in.at[i], item_send.at[i], item_recv.at[i])

    pack = Exchange(bucket, received, pack_send.at[0], pack_recv.at[0])
    late_pack = Exchange(late_bucket, late_received, pack_send.at[1], pack_recv.at[1])
    up = [Exchange(up_out.at[r], up_in.at[r], up_send.at[r], up_recv.at[r]) for r in range(rounds)]
    down = [Exchange(down_out.at[r], down_in.at[r], down_send.at[r], down_recv.at[r]) for r in range(rounds)]
    step_up = [item(r) for r in range(rounds)]
    step_down = [item(rounds + r) for r in range(rounds)]
    ask_up = [item(2 * rounds + r) for r in range(rounds)]
    ask_down = [item(3 * rounds + r) for r in range(rounds)]
    tail_up = item(4 * rounds)
    root_down = item(4 * rounds + 1)
    root_up = Exchange(root_out, root_in, root_send.at[0], root_recv.at[0])
    everything = [pack, late_pack, *up, *down, *step_up, *step_down, *ask_up, *ask_down, tail_up, root_down, root_up]

    barrier = pltpu.get_barrier_semaphore()

    @pl.loop(0, others)
    def _(k):
        pl.semaphore_signal(barrier, inc=1, device_id={"group": peer(k)}, device_id_type=pl.DeviceIdType.MESH)

    def pair(level):
        both = jnp.concatenate([to_parent[0, level], grandparent[0, level]], axis=0)
        return product(halves(both), inverses[0, level])

    def ask(r, both):
        near[r] = halves(both)
        item_out[2 * rounds + r] = jnp.concatenate([both[:rows], both[rows:]], axis=1).reshape(blocks)

    fetches[0].wait()

    spread = lax.div(lax.broadcasted_iota(jnp.int32, (nodes, rows), 1), part)
    spread = spread == lax.broadcasted_iota(jnp.int32, (nodes, rows), 0)
    spread = jnp.where(spread, 1.0, 0.0).astype(jnp.bfloat16)
    names = parents[...].astype(jnp.float32).astype(jnp.bfloat16)
    over = (((0,), (1,)), ((), ()))
    across = mm(names, spread).astype(jnp.int32)
    along = lax.dot_general(spread, names, over, preferred_element_type=jnp.float32).astype(jnp.int32)
    place_r = lax.broadcasted_iota(jnp.int32, (rows, rows), 0)
    place_c = lax.broadcasted_iota(jnp.int32, (rows, rows), 1)
    same = lax.rem(place_r, part) == lax.rem(place_c, part)
    for l in range(levels - 1):
        hit = same & (lax.div(place_r, part) == across[l : l + 1, :])
        parent_map[l] = jnp.where(hit, 1.0, 0.0).astype(jnp.bfloat16)
        hit = same & (lax.div(place_c, part) == along[:, l : l + 1])
        child_map[l] = jnp.where(hit, 1.0, 0.0).astype(jnp.bfloat16)

    for fetch in fetches[1:4]:
        fetch.wait()
    ask(0, pair(1))
    pl.semaphore_wait(barrier, others)
    ask_up[0].start()
    for fetch in fetches[4:6]:
        fetch.wait()

    dof = jnp.concatenate([gluing[i : i + 1, :] for i in range(gluing.shape[0])], axis=1)
    sign = jnp.concatenate([signs[i : i + 1, :] for i in range(signs.shape[0])], axis=1)
    coeff = (2 * sign - 1).astype(jnp.float32)
    span = levels * rows
    node = lax.div(dof, span)
    row = lax.rem(dof, span)
    order = lax.broadcasted_iota(jnp.int32, (1, count), 1)
    key = (dof * count + order).astype(jnp.float32)
    first_key = (node * (span * count)).astype(jnp.float32)
    rank = jnp.zeros((1, count), jnp.float32)
    for i in range(count // 128):
        lanes = jnp.broadcast_to(key[:, i * 128 : (i + 1) * 128], (128, 128))
        down_key = jnp.transpose(lanes)
        down_key = jnp.concatenate([down_key] * (count // 128), axis=1)
        before = (down_key < key) & (down_key >= first_key)
        rank = rank + jnp.sum(jnp.where(before, 1.0, 0.0), axis=0, keepdims=True)
    rank = rank.astype(jnp.int32)
    fits = rank < CHUNKS * SLOTS
    chunk = lax.div(rank, SLOTS)
    slot = lax.rem(rank, SLOTS)
    fine = fits & ((row >= 2 * rows) | (chunk < EARLY))
    overflow = jnp.max(jnp.where(fine, 0.0, 1.0))

    place = jnp.where(fits, node * HEAD + chunk, -1)
    owner_rows = lax.broadcasted_iota(jnp.int32, (nodes * HEAD, count), 0) == place
    low_part = jnp.where(owner_rows, lax.rem(row, rows).astype(jnp.float32), 0.0).astype(jnp.bfloat16)
    high_part = jnp.where(owner_rows, (lax.div(row, rows) * rows).astype(jnp.float32), 0.0).astype(jnp.bfloat16)
    lane_of = lax.broadcasted_iota(jnp.int32, (nodes * SLOTS, count), 0) == SLOTS * me + slot
    lane_of = jnp.where(lane_of, 1.0, 0.0).astype(jnp.bfloat16)
    contract = (((1,), (1,)), ((), ()))
    header = lax.dot_general(low_part, lane_of, contract, preferred_element_type=jnp.float32)
    header = header + lax.dot_general(high_part, lane_of, contract, preferred_element_type=jnp.float32)
    last = lax.rem(lax.broadcasted_iota(jnp.int32, header.shape, 0), HEAD) == HEAD - 1
    header = jnp.where(last, overflow, header)
    bucket[:, 0:HEAD, :] = header.reshape(nodes, HEAD, columns)

    target = jnp.where(fits, chunk * (nodes * SLOTS) + node * SLOTS + slot, -1)
    fetches[6].wait()
    m_high, m_low = split(multipliers[...])

    def packed(j):
        index = lax.broadcasted_iota(jnp.int32, (nodes * SLOTS, count), 0) + j * nodes * SLOTS
        table = jnp.where(index == target, coeff, 0.0).astype(jnp.bfloat16)
        return (mm(table, m_high) + mm(table, m_low)).reshape(nodes, SLOTS, columns)

    for j in range(EARLY):
        bucket[:, HEAD + j * SLOTS : HEAD + (j + 1) * SLOTS, :] = packed(j)
    pack.start()
    for j in range(CHUNKS - EARLY):
        late_bucket[:, j * SLOTS : (j + 1) * SLOTS, :] = packed(EARLY + j)

    ask(1, pair(3))
    last_step = product(halves(to_parent[0, levels - 2]), inverses[0, levels - 2])
    six[...] = halves(last_step)
    root_out[...] = last_step.reshape(nodes, part, rows)
    step_five[...] = pair(5)

    @pl.loop(0, levels)
    def _(l):
        inverse[l] = halves(inverses[0, l])

    def chain(a, b):
        return mm(a, b).astype(jnp.bfloat16)

    for r in range(rounds):
        w0, w1, w2 = parent_map[2 * r], parent_map[2 * r + 1], parent_map[2 * r + 2]
        near_map[r] = jnp.concatenate([w1, chain(w1, w0)], axis=1)
        both = chain(w2, w1)
        far_map[r] = jnp.concatenate([both, chain(both, w0), w2], axis=1)

    def gather(table, values):
        high, low = split(values)
        return mm(table, high) + mm(table, low)

    def answer(r):
        ask_up[r].arrived()
        found = gather(child_map[2 * r], item_in[2 * rounds + r].reshape(rows, columns))
        item_out[3 * rounds + r] = found.reshape(blocks)
        ask_down[r].start()

    def compose(r):
        ask_down[r].arrived()
        found = item_in[3 * rounds + r].reshape(rows, columns)
        found = jnp.concatenate([found[:, :rows], found[:, rows:]], axis=0)
        step = to_parent[0, 2 * r]
        leap = grandparent[0, 2 * r]
        made = product(halves(found), step)
        remote = -made[rows:]
        if r == rounds - 1:
            beyond = item_in[4 * rounds + 1].reshape(rows, columns)[:, rows:]
            remote = remote - product(halves(beyond), leap)
        far[r] = halves(jnp.concatenate([leap - made[:rows], remote, step], axis=0))

    answer(0)
    late_pack.start()
    ask_up[1].start()
    root_up.start()

    width = nodes * SLOTS

    def unpack(j, values):
        high, low = split(values.reshape(width, columns))
        rows_high[j * width : (j + 1) * width] = high
        rows_low[j * width : (j + 1) * width] = low

    def glue(level, chunks, wanted):
        table = lax.broadcasted_iota(jnp.int32, (rows, chunks * width), 0) + level * rows == wanted
        table = jnp.where(table, 1.0, 0.0).astype(jnp.bfloat16)
        glued = mm(table, rows_high[: chunks * width]) + mm(table, rows_low[: chunks * width])
        pending[level] = loads[0, level] - glued

    fetches[7].wait()
    pack.arrived()
    head = received[0, 0:HEAD, :]
    for i in range(1, nodes):
        head = head + received[i, 0:HEAD, :]
    flag[0, 0] = jnp.where(jnp.max(head[HEAD - 1 :, :]) > 0.0, 1, 0)
    wanted = jnp.concatenate([head[j : j + 1, :] for j in range(CHUNKS)], axis=1).astype(jnp.int32)
    for j in range(EARLY):
        unpack(j, received[:, HEAD + j * SLOTS : HEAD + (j + 1) * SLOTS, :])

    for l in range(2):
        glue(l, EARLY, wanted[:, : EARLY * width])

    compose(0)

    def solve(level, x):
        x = product(inverse[level], x)
        out[0, level] = x
        return x

    def skipped(r):
        step_down[r].arrived()
        solve(2 * r + 1, pending[2 * r + 1] - item_in[rounds + r].reshape(rows, columns))

    for r in range(rounds):
        level = 2 * r
        if r > 0:
            pending[level] = pending[level] - down_in[r - 1, :, :part].reshape(rows, columns)
            pending[level + 1] = pending[level + 1] - down_in[r - 1, :, part:].reshape(rows, columns)
        e = product(near[r], pending[level + 1])
        up_out[r, :, 0:part] = e[:rows].reshape(blocks)
        up_out[r, :, 2 * part : 3 * part] = e[rows:].reshape(blocks)
        x = solve(level, pending[level])
        c = product(far[r, : 2 * rows], x)
        up_out[r, :, part : 2 * part] = c[:rows].reshape(blocks)
        up_out[r, :, 3 * part :] = c[rows:].reshape(blocks)
        up[r].start()
        item_out[r] = product(far[r, 2 * rows :], x).reshape(blocks)
        step_up[r].start()

        if r == 0:
            answer(1)
            late_pack.arrived()
            for j in range(CHUNKS - EARLY):
                unpack(EARLY + j, late_received[:, j * SLOTS : (j + 1) * SLOTS, :])

            @pl.loop(2, levels)
            def _(l):
                glue(l, CHUNKS, wanted)

            root_up.arrived()
            six_in = root_in[...].reshape(rows, rows)
            above = gather(child_map[5], six_in)
            above = jnp.concatenate([above, gather(child_map[4], above)], axis=1)
            item_out[4 * rounds + 1] = above.reshape(blocks)
            root_down.start()
            item_out[4 * rounds] = product(six[...], pending[levels - 2]).reshape(blocks)
            tail_up.start()
        else:
            skipped(r - 1)
        if r == 1:
            answer(2)

        up[r].arrived()
        first = jnp.concatenate([up_in[r, :, i * part : (i + 1) * part].reshape(rows, columns) for i in (0, 1)], axis=0)
        down_out[r, :, :part] = gather(near_map[r], first).reshape(blocks)
        second = jnp.concatenate([up_in[r, :, i * part : (i + 1) * part].reshape(rows, columns) for i in (2, 3)], axis=0)
        if r == rounds - 1:
            tail_up.arrived()
            second = jnp.concatenate([second, item_in[4 * rounds].reshape(rows, columns)], axis=0)
            second = gather(far_map[r], second)
        else:
            second = gather(far_map[r, :, : 2 * rows], second)
        down_out[r, :, part:] = second.reshape(blocks)
        down[r].start()
        step_up[r].arrived()
        item_out[rounds + r] = gather(parent_map[level], item_in[r].reshape(rows, columns)).reshape(blocks)
        step_down[r].start()

        if r == 0:
            root_down.arrived()
            beyond = item_in[4 * rounds + 1].reshape(rows, columns)[:, :rows]
            five = step_five[...]
            ask(2, jnp.concatenate([five[:rows], five[rows:] - product(halves(beyond), five[:rows])], axis=0))
            ask_up[2].start()
        if r < rounds - 1:
            compose(r + 1)
        down[r].arrived()

    solve(levels - 2, pending[levels - 2] - down_in[rounds - 1, :, :part].reshape(rows, columns))
    solve(levels - 1, pending[levels - 1] - down_in[rounds - 1, :, part:].reshape(rows, columns))
    skipped(rounds - 1)

    for exchange in everything:
        exchange.sent()


def direct(loads, multipliers, gluing, signs, parents, inverses, to_parent, grandparent_factor):
    nodes = parents.shape[0]
    _, levels, rows, columns = loads.shape
    count = multipliers.shape[0]
    f32, bf16 = jnp.float32, jnp.bfloat16
    room = HEAD + EARLY * SLOTS
    rounds = levels // 2 - 1
    part = rows // nodes
    items = 4 * rounds + 2
    dma = pltpu.SemaphoreType.DMA
    vmem = pl.BlockSpec(memory_space=pltpu.VMEM)
    return pl.pallas_call(
        kernel,
        out_shape=(
            jax.ShapeDtypeStruct(loads.shape, f32),
            jax.ShapeDtypeStruct((1, 1), jnp.int32),
        ),
        in_specs=[pl.BlockSpec(memory_space=pltpu.HBM)] * 8,
        out_specs=(vmem, pl.BlockSpec(memory_space=pltpu.SMEM)),
        scratch_shapes=[
            pltpu.VMEM(loads.shape, f32),
            pltpu.VMEM(multipliers.shape, f32),
            pltpu.VMEM((count // 128, 128), jnp.int32),
            pltpu.VMEM((count // 128, 128), jnp.int32),
            pltpu.VMEM((levels - 1, nodes), jnp.int32),
            pltpu.VMEM(inverses.shape, f32),
            pltpu.VMEM(to_parent.shape, f32),
            pltpu.VMEM(grandparent_factor.shape, f32),
            dma((8,)),
            pltpu.VMEM((nodes, room, columns), f32),
            pltpu.VMEM((nodes, room, columns), f32),
            pltpu.VMEM((nodes, (CHUNKS - EARLY) * SLOTS, columns), f32),
            pltpu.VMEM((nodes, (CHUNKS - EARLY) * SLOTS, columns), f32),
            pltpu.VMEM((nodes * CHUNKS * SLOTS, columns), bf16),
            pltpu.VMEM((nodes * CHUNKS * SLOTS, columns), bf16),
            pltpu.VMEM((levels, rows, columns), f32),
            pltpu.VMEM((levels - 1, rows, rows), bf16),
            pltpu.VMEM((levels - 1, rows, rows), bf16),
            pltpu.VMEM((rounds, rows, 2 * rows), bf16),
            pltpu.VMEM((rounds, rows, 3 * rows), bf16),
            pltpu.VMEM((levels, rows, 2 * rows), bf16),
            pltpu.VMEM((rounds, 2 * rows, 2 * rows), bf16),
            pltpu.VMEM((rounds, 3 * rows, 2 * rows), bf16),
            pltpu.VMEM((rows, 2 * rows), bf16),
            pltpu.VMEM((2 * rows, rows), f32),
            pltpu.VMEM((rounds, nodes, 4 * part, columns), f32),
            pltpu.VMEM((rounds, nodes, 4 * part, columns), f32),
            pltpu.VMEM((rounds, nodes, 2 * part, columns), f32),
            pltpu.VMEM((rounds, nodes, 2 * part, columns), f32),
            pltpu.VMEM((items, nodes, part, columns), f32),
            pltpu.VMEM((items, nodes, part, columns), f32),
            pltpu.VMEM((nodes, part, rows), f32),
            pltpu.VMEM((nodes, part, rows), f32),
            dma((2,)),
            dma((2,)),
            dma((rounds,)),
            dma((rounds,)),
            dma((rounds,)),
            dma((rounds,)),
            dma((items,)),
            dma((items,)),
            dma((1,)),
            dma((1,)),
        ],
        compiler_params=pltpu.CompilerParams(
            collective_id=0, has_side_effects=True, vmem_limit_bytes=48 * 1024 * 1024
        ),
    )(
        loads,
        multipliers,
        gluing.reshape(count // 128, 128),
        signs.reshape(count // 128, 128),
        parents.T,
        inverses,
        to_parent,
        grandparent_factor,
    )


def general(loads, multipliers, gluing, signs, parents, inverses, to_parent, grandparent_factor):
    me = lax.axis_index("group")
    size = lax.axis_size("group")
    levels, rows, columns = loads.shape[1:]
    span = levels * rows
    ring = [(i, (i + 1) % size) for i in range(size)]
    exact = lax.Precision.HIGHEST

    def passed(value):
        return lax.ppermute(value, "group", ring)

    target = (me * span + lax.iota(jnp.int32, span)).astype(jnp.float32)

    def add(_, state):
        glued, values, at = state
        table = jnp.where(target[:, None] == at[None, :], 1.0, 0.0)
        glued = glued + jnp.dot(table, values, precision=exact)
        return glued, passed(values), passed(at)

    coeff = (2 * signs - 1).astype(jnp.float32)
    start = (jnp.zeros((span, columns), jnp.float32), coeff[:, None] * multipliers, gluing.astype(jnp.float32))
    glued = lax.fori_loop(0, size, add, start)[0]
    pending = loads[0] - glued.reshape(levels, rows, columns)
    pending = jnp.concatenate([pending, jnp.zeros((2, rows, columns), jnp.float32)])
    one = jnp.concatenate([to_parent[0], jnp.zeros((1, rows, rows), jnp.float32)])
    two = jnp.concatenate([grandparent_factor[0], jnp.zeros((2, rows, rows), jnp.float32)])
    firsts = jnp.concatenate([parents, jnp.zeros((size, 2), jnp.int32)], axis=1)

    def level(l, state):
        pending, solved = state
        x = jnp.dot(inverses[0, l], pending[l], precision=exact)
        solved = solved.at[l].set(x)
        first = firsts[:, l]
        second = firsts[first, l + 1]

        def take(s, state):
            here, there, up, leap = state
            source = lax.rem(me - s + size, size)
            here = here + jnp.where(first[source] == me, up, 0.0)
            there = there + jnp.where(second[source] == me, leap, 0.0)
            return here, there, passed(up), passed(leap)

        zero = jnp.zeros((rows, columns), jnp.float32)
        up = jnp.dot(one[l], x, precision=exact)
        leap = jnp.dot(two[l], x, precision=exact)
        here, there, _, _ = lax.fori_loop(0, size, take, (zero, zero, up, leap))
        return pending.at[l + 1].add(-here).at[l + 2].add(-there), solved

    solved = lax.fori_loop(0, levels, level, (pending, jnp.zeros(loads.shape[1:], jnp.float32)))[1]
    return solved[None]


def finish_kernel(source, target, done):
    pieces = [pltpu.make_async_copy(source.at[0, l], target.at[0, l], done.at[l]) for l in range(source.shape[1])]
    for piece in pieces:
        piece.start()
    for piece in pieces:
        piece.wait()


def finish(solved):
    return pl.pallas_call(
        finish_kernel,
        out_shape=jax.ShapeDtypeStruct(solved.shape, solved.dtype),
        in_specs=[pl.BlockSpec(memory_space=pltpu.VMEM)],
        out_specs=pl.BlockSpec(memory_space=pl.ANY),
        scratch_shapes=[pltpu.SemaphoreType.DMA((solved.shape[1],))],
    )(solved)


def body(*args):
    solved, flag = direct(*args)
    return lax.cond(flag[0, 0] != 0, lambda: general(*args), lambda: finish(solved))


def solution(mesh):
    return jax.shard_map(
        body,
        mesh=mesh,
        in_specs=(
            P(("cluster", "group"), None, None, None),
            P(("cluster", "group"), None),
            P(("cluster", "group")),
            P(("cluster", "group")),
            P("cluster", None),
            P(("cluster", "group"), None, None, None),
            P(("cluster", "group"), None, None, None),
            P(("cluster", "group"), None, None, None),
        ),
        out_specs=P(("cluster", "group"), None, None, None),
        check_vma=False,
    )
```

```python
import jax
import jax.numpy as jnp
from jax import lax
from jax.experimental import pallas as pl
from jax.experimental.pallas import tpu as pltpu
from jax.sharding import PartitionSpec as P

EARLY = 32
LATE = 32


def split(x):
    high = x.astype(jnp.bfloat16)
    return high, (x - high.astype(jnp.float32)).astype(jnp.bfloat16)


def mm(a, b):
    return jnp.dot(a, b, preferred_element_type=jnp.float32)


def halves(matrix):
    return jnp.concatenate(split(matrix), axis=1)


def product(matrix, x):
    high, low = split(x)
    return mm(matrix, jnp.concatenate([high, high], axis=0)) + mm(matrix[:, : matrix.shape[1] // 2], low)


def kernel(
    loads_hbm, multipliers_hbm, gluing_hbm, signs_hbm, parents_hbm, inverses_hbm, to_parent_hbm, grandparent_hbm,
    out, flag,
    loads, multipliers, gluing, signs, parents, inverses, to_parent, grandparent, fetched,
    bucket, received, late_bucket, late_received, rows_high, rows_low, pending, parent_map, child_map, near_map, far_map,
    inverse, near, far, six, step_five,
    up_out, up_in, down_out, down_in, item_out, item_in, root_out, root_in,
    pack_send, pack_recv, up_send, up_recv, down_send, down_recv, item_send, item_recv, root_send, root_recv,
):
    nodes = parents.shape[1]
    levels, rows, columns = loads.shape[1:]
    count = multipliers.shape[0]
    me = lax.axis_index("group")
    others = nodes - 1
    part = rows // nodes
    rounds = levels // 2 - 1
    blocks = (nodes, part, columns)

    arguments = (
        (parents_hbm, parents),
        (gluing_hbm, gluing),
        (signs_hbm, signs),
        (multipliers_hbm, multipliers),
        (to_parent_hbm, to_parent),
        (grandparent_hbm, grandparent),
        (inverses_hbm, inverses),
        (loads_hbm, loads),
    )
    fetches = [pltpu.make_async_copy(far, near, fetched.at[i]) for i, (far, near) in enumerate(arguments)]
    for fetch in fetches:
        fetch.start()

    def peer(k):
        def shift(t):
            return jnp.where(t < 2, t + 2, 3 - t)

        y = lax.rem(lax.div(me, 4) + shift(lax.div(k, 4)), 4)
        x = lax.rem(lax.rem(me, 4) + shift(lax.rem(k, 4)), 4)
        return 4 * y + x

    apart = [(2, 2), (2, 3), (3, 2), (2, 1), (1, 2), (3, 3), (1, 1), (3, 1), (1, 3), (0, 2), (2, 0), (0, 1), (1, 0), (0, 3), (3, 0)]
    peers = [4 * lax.rem(lax.div(me, 4) + y, 4) + lax.rem(lax.rem(me, 4) + x, 4) for y, x in apart]

    def copy(source, target, send, recv, device):
        return pltpu.make_async_remote_copy(
            src_ref=source,
            dst_ref=target,
            send_sem=send,
            recv_sem=recv,
            device_id={"group": device},
            device_id_type=pl.DeviceIdType.MESH,
        )

    class Exchange:
        def __init__(self, source, target, send, recv):
            self.source, self.target, self.send, self.recv = source, target, send, recv

        def start(self):
            for device in peers:
                copy(self.source.at[device], self.target.at[me], self.send, self.recv, device).start()
            self.target[me] = self.source[me]

        def all(self):
            most = pl.ds(0, others)
            return copy(self.source.at[most], self.target.at[most], self.send, self.recv, peer(0))

        def arrived(self):
            self.all().wait_recv()

        def sent(self):
            self.all().wait_send()

    def item(i):
        return Exchange(item_out.at[i], item_in.at[i], item_send.at[i], item_recv.at[i])

    pack = Exchange(bucket, received, pack_send.at[0], pack_recv.at[0])
    late_pack = Exchange(late_bucket, late_received, pack_send.at[1], pack_recv.at[1])
    up = [Exchange(up_out.at[r], up_in.at[r], up_send.at[r], up_recv.at[r]) for r in range(rounds)]
    down = [Exchange(down_out.at[r], down_in.at[r], down_send.at[r], down_recv.at[r]) for r in range(rounds)]
    step_up = [item(r) for r in range(rounds)]
    step_down = [item(rounds + r) for r in range(rounds)]
    ask_up = [item(2 * rounds + r) for r in range(rounds)]
    ask_down = [item(3 * rounds + r) for r in range(rounds)]
    tail_up = item(4 * rounds)
    root_down = item(4 * rounds + 1)
    root_up = Exchange(root_out, root_in, root_send.at[0], root_recv.at[0])
    everything = [pack, late_pack, *up, *down, *step_up, *step_down, *ask_up, *ask_down, tail_up, root_down, root_up]

    barrier = pltpu.get_barrier_semaphore()

    @pl.loop(0, others)
    def _(k):
        pl.semaphore_signal(barrier, inc=1, device_id={"group": peer(k)}, device_id_type=pl.DeviceIdType.MESH)

    def pair(level):
        both = jnp.concatenate([to_parent[0, level], grandparent[0, level]], axis=0)
        return product(halves(both), inverses[0, level])

    def ask(r, both):
        near[r] = halves(both)
        item_out[2 * rounds + r] = jnp.concatenate([both[:rows], both[rows:]], axis=1).reshape(blocks)

    fetches[0].wait()

    spread = lax.div(lax.broadcasted_iota(jnp.int32, (nodes, rows), 1), part)
    spread = spread == lax.broadcasted_iota(jnp.int32, (nodes, rows), 0)
    spread = jnp.where(spread, 1.0, 0.0).astype(jnp.bfloat16)
    names = parents[...].astype(jnp.float32).astype(jnp.bfloat16)
    over = (((0,), (1,)), ((), ()))
    across = mm(names, spread).astype(jnp.int32)
    along = lax.dot_general(spread, names, over, preferred_element_type=jnp.float32).astype(jnp.int32)
    place_r = lax.broadcasted_iota(jnp.int32, (rows, rows), 0)
    place_c = lax.broadcasted_iota(jnp.int32, (rows, rows), 1)
    same = lax.rem(place_r, part) == lax.rem(place_c, part)
    for l in range(levels - 1):
        hit = same & (lax.div(place_r, part) == across[l : l + 1, :])
        parent_map[l] = jnp.where(hit, 1.0, 0.0).astype(jnp.bfloat16)
        hit = same & (lax.div(place_c, part) == along[:, l : l + 1])
        child_map[l] = jnp.where(hit, 1.0, 0.0).astype(jnp.bfloat16)

    for fetch in fetches[1:3]:
        fetch.wait()

    dof = jnp.concatenate([gluing[i : i + 1, :] for i in range(gluing.shape[0])], axis=1)
    sign = jnp.concatenate([signs[i : i + 1, :] for i in range(signs.shape[0])], axis=1)
    coeff = (2 * sign - 1).astype(jnp.float32)
    span = levels * rows
    node = lax.div(dof, span)
    row = lax.rem(dof, span)
    order = lax.broadcasted_iota(jnp.int32, (1, count), 1)
    key = (dof * count + order).astype(jnp.float32)
    first_key = (node * (span * count)).astype(jnp.float32)
    rank = jnp.zeros((1, count), jnp.float32)
    for i in range(count // 128):
        lanes = jnp.broadcast_to(key[:, i * 128 : (i + 1) * 128], (128, 128))
        down_key = jnp.transpose(lanes)
        down_key = jnp.concatenate([down_key] * (count // 128), axis=1)
        before = (down_key < key) & (down_key >= first_key)
        rank = rank + jnp.sum(jnp.where(before, 1.0, 0.0), axis=0, keepdims=True)
    place = rank.astype(jnp.int32) + 1
    fine = place < jnp.where(row < 2 * rows, EARLY, EARLY + LATE)
    overflow = jnp.max(jnp.where(fine, 0.0, 1.0))

    owned = lax.broadcasted_iota(jnp.int32, (nodes, count), 0) == node
    low_part = jnp.where(owned, lax.rem(row, rows).astype(jnp.float32), 0.0).astype(jnp.bfloat16)
    high_part = jnp.where(owned, (lax.div(row, rows) * rows).astype(jnp.float32), 0.0).astype(jnp.bfloat16)
    lane_of = lax.broadcasted_iota(jnp.int32, (columns, count), 0) == place
    lane_of = jnp.where(lane_of, 1.0, 0.0).astype(jnp.bfloat16)
    contract = (((1,), (1,)), ((), ()))
    header = lax.dot_general(low_part, lane_of, contract, preferred_element_type=jnp.float32)
    header = header + lax.dot_general(high_part, lane_of, contract, preferred_element_type=jnp.float32)
    lane = lax.broadcasted_iota(jnp.int32, header.shape, 1)
    header = jnp.where(lane == 0, -1.0, jnp.where(lane < EARLY + LATE, header, overflow))

    fetches[3].wait()
    m_high, m_low = split(multipliers[...])

    def packed(first, size):
        index = lax.broadcasted_iota(jnp.int32, (nodes * size, count), 0)
        inside = (place >= first) & (place < first + size)
        table = jnp.where(index == jnp.where(inside, node * size + place - first, -1), coeff, 0.0).astype(jnp.bfloat16)
        return (mm(table, m_high) + mm(table, m_low)).reshape(nodes, size, columns)

    bucket[...] = packed(0, EARLY)
    for n in range(nodes):
        bucket[n, 0:1, :] = header[n : n + 1, :]
    for fetch in fetches[4:7]:
        fetch.wait()
    ask(0, pair(1))
    pl.semaphore_wait(barrier, others)
    ask_up[0].start()
    pack.start()
    late_bucket[...] = packed(EARLY, LATE)

    ask(1, pair(3))
    last_step = product(halves(to_parent[0, levels - 2]), inverses[0, levels - 2])
    six[...] = halves(last_step)
    root_out[...] = last_step.reshape(nodes, part, rows)
    step_five[...] = pair(5)

    @pl.loop(0, levels)
    def _(l):
        inverse[l] = halves(inverses[0, l])

    def chain(a, b):
        return mm(a, b).astype(jnp.bfloat16)

    for r in range(rounds):
        w0, w1, w2 = parent_map[2 * r], parent_map[2 * r + 1], parent_map[2 * r + 2]
        near_map[r] = jnp.concatenate([w1, chain(w1, w0)], axis=1)
        both = chain(w2, w1)
        far_map[r] = jnp.concatenate([both, chain(both, w0), w2], axis=1)

    def gather(table, values):
        high, low = split(values)
        return mm(table, high) + mm(table, low)

    def answer(r):
        ask_up[r].arrived()
        found = gather(child_map[2 * r], item_in[2 * rounds + r].reshape(rows, columns))
        item_out[3 * rounds + r] = found.reshape(blocks)
        ask_down[r].start()

    def compose(r):
        ask_down[r].arrived()
        found = item_in[3 * rounds + r].reshape(rows, columns)
        found = jnp.concatenate([found[:, :rows], found[:, rows:]], axis=0)
        step = to_parent[0, 2 * r]
        leap = grandparent[0, 2 * r]
        made = product(halves(found), step)
        remote = -made[rows:]
        if r == rounds - 1:
            beyond = item_in[4 * rounds + 1].reshape(rows, columns)[:, rows:]
            remote = remote - product(halves(beyond), leap)
        far[r] = halves(jnp.concatenate([leap - made[:rows], remote, step], axis=0))

    answer(0)
    ask_up[1].start()
    root_up.start()
    late_pack.start()

    width = nodes * EARLY

    def glue(level, wanted, source):
        table = lax.broadcasted_iota(jnp.int32, (rows, wanted.shape[1]), 0) + level * rows == wanted
        table = jnp.where(table, 1.0, 0.0).astype(jnp.bfloat16)
        return mm(table, source[0]) + mm(table, source[1])

    fetches[7].wait()
    pack.arrived()
    head = jnp.concatenate([received[n, 0:1, :] for n in range(nodes)], axis=0)
    flag[0, 0] = jnp.where(jnp.max(head[:, EARLY + LATE :]) > 0.0, 1, 0)

    def wide(first, size):
        lanes = lax.broadcasted_iota(jnp.int32, (columns, nodes * size), 1)
        pick = lax.rem(lanes, size) + first == lax.broadcasted_iota(jnp.int32, (columns, nodes * size), 0)
        pick = jnp.where(pick, 1.0, 0.0).astype(jnp.bfloat16)
        high, low = split(head)
        found = mm(high, pick) + mm(low, pick)
        sender = lax.div(lax.broadcasted_iota(jnp.int32, found.shape, 1), size)
        mine = sender == lax.broadcasted_iota(jnp.int32, found.shape, 0)
        return jnp.sum(jnp.where(mine, found, 0.0), axis=0, keepdims=True).astype(jnp.int32)

    early_rows = wide(0, EARLY)
    high, low = split(received[...].reshape(width, columns))
    rows_high[:width], rows_low[:width] = high, low
    for l in range(2):
        pending[l] = loads[0, l] - glue(l, early_rows, (high, low))

    compose(0)

    def solve(level, x):
        x = product(inverse[level], x)
        out[0, level] = x
        return x

    def skipped(r):
        step_down[r].arrived()
        solve(2 * r + 1, pending[2 * r + 1] - item_in[rounds + r].reshape(rows, columns))

    for r in range(rounds):
        level = 2 * r
        if r > 0:
            pending[level] = pending[level] - down_in[r - 1, :, :part].reshape(rows, columns)
            pending[level + 1] = pending[level + 1] - down_in[r - 1, :, part:].reshape(rows, columns)
        e = product(near[r], pending[level + 1])
        up_out[r, :, 0:part] = e[:rows].reshape(blocks)
        up_out[r, :, 2 * part : 3 * part] = e[rows:].reshape(blocks)
        x = solve(level, pending[level])
        c = product(far[r, : 2 * rows], x)
        up_out[r, :, part : 2 * part] = c[:rows].reshape(blocks)
        up_out[r, :, 3 * part :] = c[rows:].reshape(blocks)
        up[r].start()
        item_out[r] = product(far[r, 2 * rows :], x).reshape(blocks)
        step_up[r].start()

        if r == 0:
            answer(1)
            late_pack.arrived()
            every_row = jnp.concatenate([early_rows, wide(EARLY, LATE)], axis=1)
            rows_high[width:], rows_low[width:] = split(late_received[...].reshape(nodes * LATE, columns))

            @pl.loop(2, levels)
            def _(l):
                pending[l] = loads[0, l] - glue(l, every_row, (rows_high[...], rows_low[...]))

            root_up.arrived()
            six_in = root_in[...].reshape(rows, rows)
            above = gather(child_map[5], six_in)
            above = jnp.concatenate([above, gather(child_map[4], above)], axis=1)
            item_out[4 * rounds + 1] = above.reshape(blocks)
            root_down.start()
            item_out[4 * rounds] = product(six[...], pending[levels - 2]).reshape(blocks)
        else:
            skipped(r - 1)
        if r == 1:
            answer(2)

        up[r].arrived()
        first = jnp.concatenate([up_in[r, :, i * part : (i + 1) * part].reshape(rows, columns) for i in (0, 1)], axis=0)
        down_out[r, :, :part] = gather(near_map[r], first).reshape(blocks)
        second = jnp.concatenate([up_in[r, :, i * part : (i + 1) * part].reshape(rows, columns) for i in (2, 3)], axis=0)
        if r == rounds - 1:
            tail_up.arrived()
            second = jnp.concatenate([second, item_in[4 * rounds].reshape(rows, columns)], axis=0)
            second = gather(far_map[r], second)
        else:
            second = gather(far_map[r, :, : 2 * rows], second)
        down_out[r, :, part:] = second.reshape(blocks)
        down[r].start()
        if r == 1:
            tail_up.start()
        step_up[r].arrived()
        item_out[rounds + r] = gather(parent_map[level], item_in[r].reshape(rows, columns)).reshape(blocks)
        step_down[r].start()

        if r == 0:
            root_down.arrived()
            beyond = item_in[4 * rounds + 1].reshape(rows, columns)[:, :rows]
            five = step_five[...]
            ask(2, jnp.concatenate([five[:rows], five[rows:] - product(halves(beyond), five[:rows])], axis=0))
            ask_up[2].start()
        if r < rounds - 1:
            compose(r + 1)
        down[r].arrived()

    solve(levels - 2, pending[levels - 2] - down_in[rounds - 1, :, :part].reshape(rows, columns))
    solve(levels - 1, pending[levels - 1] - down_in[rounds - 1, :, part:].reshape(rows, columns))
    skipped(rounds - 1)

    for exchange in everything:
        exchange.sent()


def direct(loads, multipliers, gluing, signs, parents, inverses, to_parent, grandparent_factor):
    nodes = parents.shape[0]
    _, levels, rows, columns = loads.shape
    count = multipliers.shape[0]
    f32, bf16 = jnp.float32, jnp.bfloat16
    rounds = levels // 2 - 1
    part = rows // nodes
    items = 4 * rounds + 2
    dma = pltpu.SemaphoreType.DMA
    vmem = pl.BlockSpec(memory_space=pltpu.VMEM)
    return pl.pallas_call(
        kernel,
        out_shape=(
            jax.ShapeDtypeStruct(loads.shape, f32),
            jax.ShapeDtypeStruct((1, 1), jnp.int32),
        ),
        in_specs=[pl.BlockSpec(memory_space=pltpu.HBM)] * 8,
        out_specs=(vmem, pl.BlockSpec(memory_space=pltpu.SMEM)),
        scratch_shapes=[
            pltpu.VMEM(loads.shape, f32),
            pltpu.VMEM(multipliers.shape, f32),
            pltpu.VMEM((count // 128, 128), jnp.int32),
            pltpu.VMEM((count // 128, 128), jnp.int32),
            pltpu.VMEM((levels - 1, nodes), jnp.int32),
            pltpu.VMEM(inverses.shape, f32),
            pltpu.VMEM(to_parent.shape, f32),
            pltpu.VMEM(grandparent_factor.shape, f32),
            dma((8,)),
            pltpu.VMEM((nodes, EARLY, columns), f32),
            pltpu.VMEM((nodes, EARLY, columns), f32),
            pltpu.VMEM((nodes, LATE, columns), f32),
            pltpu.VMEM((nodes, LATE, columns), f32),
            pltpu.VMEM((nodes * (EARLY + LATE), columns), bf16),
            pltpu.VMEM((nodes * (EARLY + LATE), columns), bf16),
            pltpu.VMEM((levels, rows, columns), f32),
            pltpu.VMEM((levels - 1, rows, rows), bf16),
            pltpu.VMEM((levels - 1, rows, rows), bf16),
            pltpu.VMEM((rounds, rows, 2 * rows), bf16),
            pltpu.VMEM((rounds, rows, 3 * rows), bf16),
            pltpu.VMEM((levels, rows, 2 * rows), bf16),
            pltpu.VMEM((rounds, 2 * rows, 2 * rows), bf16),
            pltpu.VMEM((rounds, 3 * rows, 2 * rows), bf16),
            pltpu.VMEM((rows, 2 * rows), bf16),
            pltpu.VMEM((2 * rows, rows), f32),
            pltpu.VMEM((rounds, nodes, 4 * part, columns), f32),
            pltpu.VMEM((rounds, nodes, 4 * part, columns), f32),
            pltpu.VMEM((rounds, nodes, 2 * part, columns), f32),
            pltpu.VMEM((rounds, nodes, 2 * part, columns), f32),
            pltpu.VMEM((items, nodes, part, columns), f32),
            pltpu.VMEM((items, nodes, part, columns), f32),
            pltpu.VMEM((nodes, part, rows), f32),
            pltpu.VMEM((nodes, part, rows), f32),
            dma((2,)),
            dma((2,)),
            dma((rounds,)),
            dma((rounds,)),
            dma((rounds,)),
            dma((rounds,)),
            dma((items,)),
            dma((items,)),
            dma((1,)),
            dma((1,)),
        ],
        compiler_params=pltpu.CompilerParams(
            collective_id=0, has_side_effects=True, vmem_limit_bytes=48 * 1024 * 1024
        ),
    )(
        loads,
        multipliers,
        gluing.reshape(count // 128, 128),
        signs.reshape(count // 128, 128),
        parents.T,
        inverses,
        to_parent,
        grandparent_factor,
    )


def general(loads, multipliers, gluing, signs, parents, inverses, to_parent, grandparent_factor):
    me = lax.axis_index("group")
    size = lax.axis_size("group")
    levels, rows, columns = loads.shape[1:]
    span = levels * rows
    ring = [(i, (i + 1) % size) for i in range(size)]
    exact = lax.Precision.HIGHEST

    def passed(value):
        return lax.ppermute(value, "group", ring)

    target = (me * span + lax.iota(jnp.int32, span)).astype(jnp.float32)

    def add(_, state):
        glued, values, at = state
        table = jnp.where(target[:, None] == at[None, :], 1.0, 0.0)
        glued = glued + jnp.dot(table, values, precision=exact)
        return glued, passed(values), passed(at)

    coeff = (2 * signs - 1).astype(jnp.float32)
    start = (jnp.zeros((span, columns), jnp.float32), coeff[:, None] * multipliers, gluing.astype(jnp.float32))
    glued = lax.fori_loop(0, size, add, start)[0]
    pending = loads[0] - glued.reshape(levels, rows, columns)
    pending = jnp.concatenate([pending, jnp.zeros((2, rows, columns), jnp.float32)])
    one = jnp.concatenate([to_parent[0], jnp.zeros((1, rows, rows), jnp.float32)])
    two = jnp.concatenate([grandparent_factor[0], jnp.zeros((2, rows, rows), jnp.float32)])
    firsts = jnp.concatenate([parents, jnp.zeros((size, 2), jnp.int32)], axis=1)

    def level(l, state):
        pending, solved = state
        x = jnp.dot(inverses[0, l], pending[l], precision=exact)
        solved = solved.at[l].set(x)
        first = firsts[:, l]
        second = firsts[first, l + 1]

        def take(s, state):
            here, there, up, leap = state
            source = lax.rem(me - s + size, size)
            here = here + jnp.where(first[source] == me, up, 0.0)
            there = there + jnp.where(second[source] == me, leap, 0.0)
            return here, there, passed(up), passed(leap)

        zero = jnp.zeros((rows, columns), jnp.float32)
        up = jnp.dot(one[l], x, precision=exact)
        leap = jnp.dot(two[l], x, precision=exact)
        here, there, _, _ = lax.fori_loop(0, size, take, (zero, zero, up, leap))
        return pending.at[l + 1].add(-here).at[l + 2].add(-there), solved

    solved = lax.fori_loop(0, levels, level, (pending, jnp.zeros(loads.shape[1:], jnp.float32)))[1]
    return solved[None]


def finish_kernel(source, target, done):
    pieces = [pltpu.make_async_copy(source.at[0, l], target.at[0, l], done.at[l]) for l in range(source.shape[1])]
    for piece in pieces:
        piece.start()
    for piece in pieces:
        piece.wait()


def finish(solved):
    return pl.pallas_call(
        finish_kernel,
        out_shape=jax.ShapeDtypeStruct(solved.shape, solved.dtype),
        in_specs=[pl.BlockSpec(memory_space=pltpu.VMEM)],
        out_specs=pl.BlockSpec(memory_space=pl.ANY),
        scratch_shapes=[pltpu.SemaphoreType.DMA((solved.shape[1],))],
    )(solved)


def body(*args):
    solved, flag = direct(*args)
    return lax.cond(flag[0, 0] != 0, lambda: general(*args), lambda: finish(solved))


def solution(mesh):
    return jax.shard_map(
        body,
        mesh=mesh,
        in_specs=(
            P(("cluster", "group"), None, None, None),
            P(("cluster", "group"), None),
            P(("cluster", "group")),
            P(("cluster", "group")),
            P("cluster", None),
            P(("cluster", "group"), None, None, None),
            P(("cluster", "group"), None, None, None),
            P(("cluster", "group"), None, None, None),
        ),
        out_specs=P(("cluster", "group"), None, None, None),
        check_vma=False,
    )
```

```python
import jax
import jax.numpy as jnp
from jax import lax
from jax.experimental import pallas as pl
from jax.experimental.pallas import tpu as pltpu
from jax.sharding import PartitionSpec as P

EARLY = 32
LATE = 32
PIECE = 16


def split(x):
    high = x.astype(jnp.bfloat16)
    return high, (x - high.astype(jnp.float32)).astype(jnp.bfloat16)


def mm(a, b):
    return jnp.dot(a, b, preferred_element_type=jnp.float32)


def halves(matrix):
    return jnp.concatenate(split(matrix), axis=1)


def product(matrix, x):
    high, low = split(x)
    return mm(matrix, jnp.concatenate([high, high], axis=0)) + mm(matrix[:, : matrix.shape[1] // 2], low)


def kernel(
    loads_hbm, multipliers_hbm, gluing_hbm, signs_hbm, parents_hbm, inverses_hbm, to_parent_hbm, grandparent_hbm,
    out, flag,
    loads, multipliers, gluing, signs, parents, inverses, to_parent, grandparent, fetched,
    bucket, received, late_bucket, late_received, rows_high, rows_low, pending, parent_map, child_map, near_map, far_map,
    inverse, near, far, six, step_five, own,
    up_out, up_in, down_out, down_in, item_out, item_in, root_out, root_in,
    pack_send, pack_recv, up_send, up_recv, down_send, down_recv, item_send, item_recv, root_send, root_recv,
):
    nodes = parents.shape[1]
    levels, rows, columns = loads.shape[1:]
    count = multipliers.shape[0]
    me = lax.axis_index("group")
    others = nodes - 1
    part = rows // nodes
    rounds = levels // 2 - 1
    blocks = (nodes, part, columns)

    arguments = (
        (parents_hbm, parents),
        (to_parent_hbm, to_parent),
        (grandparent_hbm, grandparent),
        (inverses_hbm, inverses),
        (gluing_hbm, gluing),
        (signs_hbm, signs),
        (multipliers_hbm, multipliers),
        (loads_hbm, loads),
    )
    fetches = [pltpu.make_async_copy(far, near, fetched.at[i]) for i, (far, near) in enumerate(arguments)]
    for fetch in fetches:
        fetch.start()

    def peer(k):
        def shift(t):
            return jnp.where(t < 2, t + 2, 3 - t)

        y = lax.rem(lax.div(me, 4) + shift(lax.div(k, 4)), 4)
        x = lax.rem(lax.rem(me, 4) + shift(lax.rem(k, 4)), 4)
        return 4 * y + x

    apart = [(2, 2), (2, 3), (3, 2), (2, 1), (1, 2), (3, 3), (1, 1), (3, 1), (1, 3), (0, 2), (2, 0), (0, 1), (1, 0), (0, 3), (3, 0)]
    peers = [4 * lax.rem(lax.div(me, 4) + y, 4) + lax.rem(lax.rem(me, 4) + x, 4) for y, x in apart]

    def copy(source, target, send, recv, device):
        return pltpu.make_async_remote_copy(
            src_ref=source,
            dst_ref=target,
            send_sem=send,
            recv_sem=recv,
            device_id={"group": device},
            device_id_type=pl.DeviceIdType.MESH,
        )

    class Exchange:
        def __init__(self, source, target, send, recv):
            self.source, self.target, self.send, self.recv = source, target, send, recv

        def start(self):
            high = self.source.shape[1]
            for first in range(0, high, PIECE):
                here = pl.ds(first, min(PIECE, high))
                for device in peers:
                    copy(self.source.at[device, here], self.target.at[me, here], self.send, self.recv, device).start()
            self.target[me] = self.source[me]

        def all(self):
            most = pl.ds(0, others)
            return copy(self.source.at[most], self.target.at[most], self.send, self.recv, peer(0))

        def arrived(self):
            self.all().wait_recv()

        def sent(self):
            self.all().wait_send()

    def item(i):
        return Exchange(item_out.at[i], item_in.at[i], item_send.at[i], item_recv.at[i])

    pack = Exchange(bucket, received, pack_send.at[0], pack_recv.at[0])
    late_pack = Exchange(late_bucket, late_received, pack_send.at[1], pack_recv.at[1])
    up = [Exchange(up_out.at[r], up_in.at[r], up_send.at[r], up_recv.at[r]) for r in range(rounds)]
    down = [Exchange(down_out.at[r], down_in.at[r], down_send.at[r], down_recv.at[r]) for r in range(rounds)]
    step_up = [item(r) for r in range(rounds)]
    step_down = [item(rounds + r) for r in range(rounds)]
    ask_up = [item(2 * rounds + r) for r in range(rounds)]
    ask_down = [item(3 * rounds + r) for r in range(rounds)]
    tail_up = item(4 * rounds)
    root_down = item(4 * rounds + 1)
    root_up = Exchange(root_out, root_in, root_send.at[0], root_recv.at[0])
    everything = [pack, late_pack, *up, *down, *step_up, *step_down, *ask_up, *ask_down, tail_up, root_down, root_up]

    barrier = pltpu.get_barrier_semaphore()

    @pl.loop(0, others)
    def _(k):
        pl.semaphore_signal(barrier, inc=1, device_id={"group": peer(k)}, device_id_type=pl.DeviceIdType.MESH)

    def pair(level):
        both = jnp.concatenate([to_parent[0, level], grandparent[0, level]], axis=0)
        return product(halves(both), inverses[0, level])

    def ask(r, both):
        near[r] = halves(both)
        item_out[2 * rounds + r] = jnp.concatenate([both[:rows], both[rows:]], axis=1).reshape(blocks)

    fetches[0].wait()

    spread = lax.div(lax.broadcasted_iota(jnp.int32, (nodes, rows), 1), part)
    spread = spread == lax.broadcasted_iota(jnp.int32, (nodes, rows), 0)
    spread = jnp.where(spread, 1.0, 0.0).astype(jnp.bfloat16)
    names = parents[...].astype(jnp.float32).astype(jnp.bfloat16)
    over = (((0,), (1,)), ((), ()))
    across = mm(names, spread).astype(jnp.int32)
    along = lax.dot_general(spread, names, over, preferred_element_type=jnp.float32).astype(jnp.int32)
    place_r = lax.broadcasted_iota(jnp.int32, (rows, rows), 0)
    place_c = lax.broadcasted_iota(jnp.int32, (rows, rows), 1)
    same = lax.rem(place_r, part) == lax.rem(place_c, part)
    for l in range(levels - 1):
        hit = same & (lax.div(place_r, part) == across[l : l + 1, :])
        parent_map[l] = jnp.where(hit, 1.0, 0.0).astype(jnp.bfloat16)
        hit = same & (lax.div(place_c, part) == along[:, l : l + 1])
        child_map[l] = jnp.where(hit, 1.0, 0.0).astype(jnp.bfloat16)

    for fetch in fetches[1:4]:
        fetch.wait()
    ask(0, pair(1))
    ask(1, pair(3))
    last_step = product(halves(to_parent[0, levels - 2]), inverses[0, levels - 2])
    six[...] = halves(last_step)
    root_out[...] = last_step.reshape(nodes, part, rows)
    pl.semaphore_wait(barrier, others)
    ask_up[0].start()
    ask_up[1].start()
    root_up.start()
    for fetch in fetches[4:6]:
        fetch.wait()

    dof = jnp.concatenate([gluing[i : i + 1, :] for i in range(gluing.shape[0])], axis=1)
    sign = jnp.concatenate([signs[i : i + 1, :] for i in range(signs.shape[0])], axis=1)
    coeff = (2 * sign - 1).astype(jnp.float32)
    span = levels * rows
    node = lax.div(dof, span)
    row = lax.rem(dof, span)
    order = lax.broadcasted_iota(jnp.int32, (1, count), 1)
    key = (dof * count + order).astype(jnp.float32)
    first_key = (node * (span * count)).astype(jnp.float32)
    rank = jnp.zeros((1, count), jnp.float32)
    for i in range(count // 128):
        lanes = jnp.broadcast_to(key[:, i * 128 : (i + 1) * 128], (128, 128))
        down_key = jnp.transpose(lanes)
        down_key = jnp.concatenate([down_key] * (count // 128), axis=1)
        before = (down_key < key) & (down_key >= first_key)
        rank = rank + jnp.sum(jnp.where(before, 1.0, 0.0), axis=0, keepdims=True)
    place = rank.astype(jnp.int32) + 1
    fine = place < jnp.where(row < 2 * rows, EARLY, EARLY + LATE)
    overflow = jnp.max(jnp.where(fine, 0.0, 1.0))

    owned = lax.broadcasted_iota(jnp.int32, (nodes, count), 0) == node
    low_part = jnp.where(owned, lax.rem(row, rows).astype(jnp.float32), 0.0).astype(jnp.bfloat16)
    high_part = jnp.where(owned, (lax.div(row, rows) * rows).astype(jnp.float32), 0.0).astype(jnp.bfloat16)
    lane_of = lax.broadcasted_iota(jnp.int32, (columns, count), 0) == place
    lane_of = jnp.where(lane_of, 1.0, 0.0).astype(jnp.bfloat16)
    contract = (((1,), (1,)), ((), ()))
    header = lax.dot_general(low_part, lane_of, contract, preferred_element_type=jnp.float32)
    header = header + lax.dot_general(high_part, lane_of, contract, preferred_element_type=jnp.float32)
    lane = lax.broadcasted_iota(jnp.int32, header.shape, 1)
    header = jnp.where(lane == 0, -1.0, jnp.where(lane < EARLY + LATE, header, overflow))

    fetches[6].wait()
    m_high, m_low = split(multipliers[...])

    def packed(first, size):
        index = lax.broadcasted_iota(jnp.int32, (nodes * size, count), 0)
        inside = (place >= first) & (place < first + size)
        table = jnp.where(index == jnp.where(inside, node * size + place - first, -1), coeff, 0.0).astype(jnp.bfloat16)
        return (mm(table, m_high) + mm(table, m_low)).reshape(nodes, size, columns)

    bucket[...] = packed(0, EARLY)
    for n in range(nodes):
        bucket[n, 0:1, :] = header[n : n + 1, :]
    pack.start()
    late_bucket[...] = packed(EARLY, LATE)

    own[0] = pair(0)

    @pl.loop(0, levels)
    def _(l):
        inverse[l] = halves(inverses[0, l])

    def chain(a, b):
        return mm(a, b).astype(jnp.bfloat16)

    for r in range(rounds):
        w0, w1, w2 = parent_map[2 * r], parent_map[2 * r + 1], parent_map[2 * r + 2]
        near_map[r] = jnp.concatenate([w1, chain(w1, w0)], axis=1)
        both = chain(w2, w1)
        far_map[r] = jnp.concatenate([both, chain(both, w0), w2], axis=1)

    def gather(table, values):
        high, low = split(values)
        return mm(table, high) + mm(table, low)

    def answer(r):
        ask_up[r].arrived()
        found = gather(child_map[2 * r], item_in[2 * rounds + r].reshape(rows, columns))
        item_out[3 * rounds + r] = found.reshape(blocks)
        ask_down[r].start()

    def compose(r):
        ask_down[r].arrived()
        found = item_in[3 * rounds + r].reshape(rows, columns)
        found = jnp.concatenate([found[:, :rows], found[:, rows:]], axis=0)
        step = own[r, :rows]
        leap = own[r, rows:]
        made = product(halves(found), step)
        remote = -made[rows:]
        if r == rounds - 1:
            beyond = item_in[4 * rounds + 1].reshape(rows, columns)[:, rows:]
            remote = remote - product(halves(beyond), leap)
        far[r] = halves(jnp.concatenate([leap - made[:rows], remote, step], axis=0))

    answer(0)
    late_pack.start()

    width = nodes * EARLY

    def glue(level, wanted, source):
        table = lax.broadcasted_iota(jnp.int32, (rows, wanted.shape[1]), 0) + level * rows == wanted
        table = jnp.where(table, 1.0, 0.0).astype(jnp.bfloat16)
        return mm(table, source[0]) + mm(table, source[1])

    fetches[7].wait()
    pack.arrived()
    head = jnp.concatenate([received[n, 0:1, :] for n in range(nodes)], axis=0)
    flag[0, 0] = jnp.where(jnp.max(head[:, EARLY + LATE :]) > 0.0, 1, 0)

    def wide(first, size):
        lanes = lax.broadcasted_iota(jnp.int32, (columns, nodes * size), 1)
        pick = lax.rem(lanes, size) + first == lax.broadcasted_iota(jnp.int32, (columns, nodes * size), 0)
        pick = jnp.where(pick, 1.0, 0.0).astype(jnp.bfloat16)
        high, low = split(head)
        found = mm(high, pick) + mm(low, pick)
        sender = lax.div(lax.broadcasted_iota(jnp.int32, found.shape, 1), size)
        mine = sender == lax.broadcasted_iota(jnp.int32, found.shape, 0)
        return jnp.sum(jnp.where(mine, found, 0.0), axis=0, keepdims=True).astype(jnp.int32)

    early_rows = wide(0, EARLY)
    high, low = split(received[...].reshape(width, columns))
    rows_high[:width], rows_low[:width] = high, low
    for l in range(2):
        pending[l] = loads[0, l] - glue(l, early_rows, (high, low))

    compose(0)

    def solve(level, x):
        out[0, level] = product(inverse[level], x)

    def skipped(r):
        step_down[r].arrived()
        solve(2 * r + 1, pending[2 * r + 1] - item_in[rounds + r].reshape(rows, columns))

    for r in range(rounds):
        level = 2 * r
        if r > 0:
            pending[level] = pending[level] - down_in[r - 1, :, :part].reshape(rows, columns)
            pending[level + 1] = pending[level + 1] - down_in[r - 1, :, part:].reshape(rows, columns)
        e = product(near[r], pending[level + 1])
        up_out[r, :, 0:part] = e[:rows].reshape(blocks)
        up_out[r, :, 2 * part : 3 * part] = e[rows:].reshape(blocks)
        c = product(far[r, : 2 * rows], pending[level])
        up_out[r, :, part : 2 * part] = c[:rows].reshape(blocks)
        up_out[r, :, 3 * part :] = c[rows:].reshape(blocks)
        up[r].start()
        item_out[r] = product(far[r, 2 * rows :], pending[level]).reshape(blocks)
        step_up[r].start()
        solve(level, pending[level])

        if r == 0:
            step_five[...] = pair(5)
            for later in range(1, rounds):
                own[later] = pair(2 * later)
            answer(1)
            late_pack.arrived()
            every_row = jnp.concatenate([early_rows, wide(EARLY, LATE)], axis=1)
            rows_high[width:], rows_low[width:] = split(late_received[...].reshape(nodes * LATE, columns))

            @pl.loop(2, levels)
            def _(l):
                pending[l] = loads[0, l] - glue(l, every_row, (rows_high[...], rows_low[...]))

            root_up.arrived()
            six_in = root_in[...].reshape(rows, rows)
            above = gather(child_map[5], six_in)
            above = jnp.concatenate([above, gather(child_map[4], above)], axis=1)
            item_out[4 * rounds + 1] = above.reshape(blocks)
            root_down.start()
            item_out[4 * rounds] = product(six[...], pending[levels - 2]).reshape(blocks)
        else:
            skipped(r - 1)
        if r == 1:
            answer(2)

        up[r].arrived()
        first = jnp.concatenate([up_in[r, :, i * part : (i + 1) * part].reshape(rows, columns) for i in (0, 1)], axis=0)
        down_out[r, :, :part] = gather(near_map[r], first).reshape(blocks)
        second = jnp.concatenate([up_in[r, :, i * part : (i + 1) * part].reshape(rows, columns) for i in (2, 3)], axis=0)
        if r == rounds - 1:
            tail_up.arrived()
            second = jnp.concatenate([second, item_in[4 * rounds].reshape(rows, columns)], axis=0)
            second = gather(far_map[r], second)
        else:
            second = gather(far_map[r, :, : 2 * rows], second)
        down_out[r, :, part:] = second.reshape(blocks)
        down[r].start()
        if r == 1:
            tail_up.start()
        step_up[r].arrived()
        item_out[rounds + r] = gather(parent_map[level], item_in[r].reshape(rows, columns)).reshape(blocks)
        step_down[r].start()

        if r == 0:
            root_down.arrived()
            beyond = item_in[4 * rounds + 1].reshape(rows, columns)[:, :rows]
            five = step_five[...]
            ask(2, jnp.concatenate([five[:rows], five[rows:] - product(halves(beyond), five[:rows])], axis=0))
            ask_up[2].start()
        if r < rounds - 1:
            compose(r + 1)
        down[r].arrived()

    solve(levels - 2, pending[levels - 2] - down_in[rounds - 1, :, :part].reshape(rows, columns))
    solve(levels - 1, pending[levels - 1] - down_in[rounds - 1, :, part:].reshape(rows, columns))
    skipped(rounds - 1)

    for exchange in everything:
        exchange.sent()


def direct(loads, multipliers, gluing, signs, parents, inverses, to_parent, grandparent_factor):
    nodes = parents.shape[0]
    _, levels, rows, columns = loads.shape
    count = multipliers.shape[0]
    f32, bf16 = jnp.float32, jnp.bfloat16
    rounds = levels // 2 - 1
    part = rows // nodes
    items = 4 * rounds + 2
    dma = pltpu.SemaphoreType.DMA
    vmem = pl.BlockSpec(memory_space=pltpu.VMEM)
    return pl.pallas_call(
        kernel,
        out_shape=(
            jax.ShapeDtypeStruct(loads.shape, f32),
            jax.ShapeDtypeStruct((1, 1), jnp.int32),
        ),
        in_specs=[pl.BlockSpec(memory_space=pltpu.HBM)] * 8,
        out_specs=(vmem, pl.BlockSpec(memory_space=pltpu.SMEM)),
        scratch_shapes=[
            pltpu.VMEM(loads.shape, f32),
            pltpu.VMEM(multipliers.shape, f32),
            pltpu.VMEM((count // 128, 128), jnp.int32),
            pltpu.VMEM((count // 128, 128), jnp.int32),
            pltpu.VMEM((levels - 1, nodes), jnp.int32),
            pltpu.VMEM(inverses.shape, f32),
            pltpu.VMEM(to_parent.shape, f32),
            pltpu.VMEM(grandparent_factor.shape, f32),
            dma((8,)),
            pltpu.VMEM((nodes, EARLY, columns), f32),
            pltpu.VMEM((nodes, EARLY, columns), f32),
            pltpu.VMEM((nodes, LATE, columns), f32),
            pltpu.VMEM((nodes, LATE, columns), f32),
            pltpu.VMEM((nodes * (EARLY + LATE), columns), bf16),
            pltpu.VMEM((nodes * (EARLY + LATE), columns), bf16),
            pltpu.VMEM((levels, rows, columns), f32),
            pltpu.VMEM((levels - 1, rows, rows), bf16),
            pltpu.VMEM((levels - 1, rows, rows), bf16),
            pltpu.VMEM((rounds, rows, 2 * rows), bf16),
            pltpu.VMEM((rounds, rows, 3 * rows), bf16),
            pltpu.VMEM((levels, rows, 2 * rows), bf16),
            pltpu.VMEM((rounds, 2 * rows, 2 * rows), bf16),
            pltpu.VMEM((rounds, 3 * rows, 2 * rows), bf16),
            pltpu.VMEM((rows, 2 * rows), bf16),
            pltpu.VMEM((2 * rows, rows), f32),
            pltpu.VMEM((rounds, 2 * rows, rows), f32),
            pltpu.VMEM((rounds, nodes, 4 * part, columns), f32),
            pltpu.VMEM((rounds, nodes, 4 * part, columns), f32),
            pltpu.VMEM((rounds, nodes, 2 * part, columns), f32),
            pltpu.VMEM((rounds, nodes, 2 * part, columns), f32),
            pltpu.VMEM((items, nodes, part, columns), f32),
            pltpu.VMEM((items, nodes, part, columns), f32),
            pltpu.VMEM((nodes, part, rows), f32),
            pltpu.VMEM((nodes, part, rows), f32),
            dma((2,)),
            dma((2,)),
            dma((rounds,)),
            dma((rounds,)),
            dma((rounds,)),
            dma((rounds,)),
            dma((items,)),
            dma((items,)),
            dma((1,)),
            dma((1,)),
        ],
        compiler_params=pltpu.CompilerParams(
            collective_id=0, has_side_effects=True, vmem_limit_bytes=48 * 1024 * 1024
        ),
    )(
        loads,
        multipliers,
        gluing.reshape(count // 128, 128),
        signs.reshape(count // 128, 128),
        parents.T,
        inverses,
        to_parent,
        grandparent_factor,
    )


def general(loads, multipliers, gluing, signs, parents, inverses, to_parent, grandparent_factor):
    me = lax.axis_index("group")
    size = lax.axis_size("group")
    levels, rows, columns = loads.shape[1:]
    span = levels * rows
    ring = [(i, (i + 1) % size) for i in range(size)]
    exact = lax.Precision.HIGHEST

    def passed(value):
        return lax.ppermute(value, "group", ring)

    target = (me * span + lax.iota(jnp.int32, span)).astype(jnp.float32)

    def add(_, state):
        glued, values, at = state
        table = jnp.where(target[:, None] == at[None, :], 1.0, 0.0)
        glued = glued + jnp.dot(table, values, precision=exact)
        return glued, passed(values), passed(at)

    coeff = (2 * signs - 1).astype(jnp.float32)
    start = (jnp.zeros((span, columns), jnp.float32), coeff[:, None] * multipliers, gluing.astype(jnp.float32))
    glued = lax.fori_loop(0, size, add, start)[0]
    pending = loads[0] - glued.reshape(levels, rows, columns)
    pending = jnp.concatenate([pending, jnp.zeros((2, rows, columns), jnp.float32)])
    one = jnp.concatenate([to_parent[0], jnp.zeros((1, rows, rows), jnp.float32)])
    two = jnp.concatenate([grandparent_factor[0], jnp.zeros((2, rows, rows), jnp.float32)])
    firsts = jnp.concatenate([parents, jnp.zeros((size, 2), jnp.int32)], axis=1)

    def level(l, state):
        pending, solved = state
        x = jnp.dot(inverses[0, l], pending[l], precision=exact)
        solved = solved.at[l].set(x)
        first = firsts[:, l]
        second = firsts[first, l + 1]

        def take(s, state):
            here, there, up, leap = state
            source = lax.rem(me - s + size, size)
            here = here + jnp.where(first[source] == me, up, 0.0)
            there = there + jnp.where(second[source] == me, leap, 0.0)
            return here, there, passed(up), passed(leap)

        zero = jnp.zeros((rows, columns), jnp.float32)
        up = jnp.dot(one[l], x, precision=exact)
        leap = jnp.dot(two[l], x, precision=exact)
        here, there, _, _ = lax.fori_loop(0, size, take, (zero, zero, up, leap))
        return pending.at[l + 1].add(-here).at[l + 2].add(-there), solved

    solved = lax.fori_loop(0, levels, level, (pending, jnp.zeros(loads.shape[1:], jnp.float32)))[1]
    return solved[None]


def finish_kernel(source, target, done):
    pieces = [pltpu.make_async_copy(source.at[0, l], target.at[0, l], done.at[l]) for l in range(source.shape[1])]
    for piece in pieces:
        piece.start()
    for piece in pieces:
        piece.wait()


def finish(solved):
    return pl.pallas_call(
        finish_kernel,
        out_shape=jax.ShapeDtypeStruct(solved.shape, solved.dtype),
        in_specs=[pl.BlockSpec(memory_space=pltpu.VMEM)],
        out_specs=pl.BlockSpec(memory_space=pl.ANY),
        scratch_shapes=[pltpu.SemaphoreType.DMA((solved.shape[1],))],
    )(solved)


def body(*args):
    solved, flag = direct(*args)
    return lax.switch(flag[0, 0], (lambda: finish(solved), lambda: general(*args)))


def solution(mesh):
    return jax.shard_map(
        body,
        mesh=mesh,
        in_specs=(
            P(("cluster", "group"), None, None, None),
            P(("cluster", "group"), None),
            P(("cluster", "group")),
            P(("cluster", "group")),
            P("cluster", None),
            P(("cluster", "group"), None, None, None),
            P(("cluster", "group"), None, None, None),
            P(("cluster", "group"), None, None, None),
        ),
        out_specs=P(("cluster", "group"), None, None, None),
        check_vma=False,
    )
```

```python
import jax
import jax.numpy as jnp
from jax import lax
from jax.experimental import pallas as pl
from jax.experimental.pallas import tpu as pltpu
from jax.sharding import PartitionSpec as P

EARLY = 32
LATE = 32
PIECE = 16


def split(x):
    high = x.astype(jnp.bfloat16)
    return high, (x - high.astype(jnp.float32)).astype(jnp.bfloat16)


def mm(a, b):
    return jnp.dot(a, b, preferred_element_type=jnp.float32)


def halves(matrix):
    return jnp.concatenate(split(matrix), axis=1)


def product(matrix, x):
    high, low = split(x)
    return mm(matrix, jnp.concatenate([high, high], axis=0)) + mm(matrix[:, : matrix.shape[1] // 2], low)


def kernel(
    loads_hbm, multipliers_hbm, gluing_hbm, signs_hbm, parents_hbm, inverses_hbm, to_parent_hbm, grandparent_hbm,
    out, flag,
    loads, multipliers, gluing, signs, parents, inverses, to_parent, grandparent, fetched,
    bucket, received, late_bucket, late_received, rows_high, rows_low, pending, parent_map, child_map, near_map, far_map,
    inverse, near, far, six, step_five, own,
    up_out, up_in, down_out, down_in, item_out, item_in, root_out, root_in,
    pack_send, pack_recv, up_send, up_recv, down_send, down_recv, item_send, item_recv, root_send, root_recv,
):
    nodes = parents.shape[1]
    levels, rows, columns = loads.shape[1:]
    count = multipliers.shape[0]
    me = lax.axis_index("group")
    others = nodes - 1
    part = rows // nodes
    rounds = levels // 2 - 1
    blocks = (nodes, part, columns)

    arguments = (
        (parents_hbm, parents),
        (to_parent_hbm, to_parent),
        (grandparent_hbm, grandparent),
        (inverses_hbm, inverses),
        (gluing_hbm, gluing),
        (signs_hbm, signs),
        (multipliers_hbm, multipliers),
        (loads_hbm, loads),
    )
    fetches = [pltpu.make_async_copy(far, near, fetched.at[i]) for i, (far, near) in enumerate(arguments)]
    for fetch in fetches:
        fetch.start()

    def peer(k):
        def shift(t):
            return jnp.where(t < 2, t + 2, 3 - t)

        y = lax.rem(lax.div(me, 4) + shift(lax.div(k, 4)), 4)
        x = lax.rem(lax.rem(me, 4) + shift(lax.rem(k, 4)), 4)
        return 4 * y + x

    apart = [(2, 2), (2, 3), (3, 2), (2, 1), (1, 2), (3, 3), (1, 1), (3, 1), (1, 3), (0, 2), (2, 0), (0, 1), (1, 0), (0, 3), (3, 0)]
    peers = [4 * lax.rem(lax.div(me, 4) + y, 4) + lax.rem(lax.rem(me, 4) + x, 4) for y, x in apart]

    def copy(source, target, send, recv, device):
        return pltpu.make_async_remote_copy(
            src_ref=source,
            dst_ref=target,
            send_sem=send,
            recv_sem=recv,
            device_id={"group": device},
            device_id_type=pl.DeviceIdType.MESH,
        )

    class Exchange:
        def __init__(self, source, target, send, recv):
            self.source, self.target, self.send, self.recv = source, target, send, recv

        def start(self):
            for first in range(0, self.source.shape[1], PIECE):
                self.start_piece(first)

        def start_piece(self, first):
            size = min(PIECE, self.source.shape[1])
            here = pl.ds(first, size)
            for device in peers:
                copy(self.source.at[device, here], self.target.at[me, here], self.send, self.recv, device).start()
            self.target[me, first : first + size] = self.source[me, first : first + size]

        def all(self):
            most = pl.ds(0, others)
            return copy(self.source.at[most], self.target.at[most], self.send, self.recv, peer(0))

        def arrived(self):
            self.all().wait_recv()

        def sent(self):
            self.all().wait_send()

    def item(i):
        return Exchange(item_out.at[i], item_in.at[i], item_send.at[i], item_recv.at[i])

    pack = Exchange(bucket, received, pack_send.at[0], pack_recv.at[0])
    late_pack = Exchange(late_bucket, late_received, pack_send.at[1], pack_recv.at[1])
    up = [Exchange(up_out.at[r], up_in.at[r], up_send.at[r], up_recv.at[r]) for r in range(rounds)]
    down = [Exchange(down_out.at[r], down_in.at[r], down_send.at[r], down_recv.at[r]) for r in range(2 * rounds)]
    step_up = [item(r) for r in range(rounds)]
    step_down = [item(rounds + r) for r in range(rounds)]
    ask_up = [item(2 * rounds + r) for r in range(rounds)]
    ask_down = [item(3 * rounds + r) for r in range(rounds)]
    tail_up = item(4 * rounds)
    root_down = item(4 * rounds + 1)
    root_up = Exchange(root_out, root_in, root_send.at[0], root_recv.at[0])
    everything = [pack, late_pack, *up, *down, *step_up, *step_down, *ask_up, *ask_down, tail_up, root_down, root_up]

    barrier = pltpu.get_barrier_semaphore()

    @pl.loop(0, others)
    def _(k):
        pl.semaphore_signal(barrier, inc=1, device_id={"group": peer(k)}, device_id_type=pl.DeviceIdType.MESH)

    def pair(level):
        both = jnp.concatenate([to_parent[0, level], grandparent[0, level]], axis=0)
        return product(halves(both), inverses[0, level])

    def ask(r, both):
        near[r] = halves(both)
        item_out[2 * rounds + r] = jnp.concatenate([both[:rows], both[rows:]], axis=1).reshape(blocks)

    fetches[0].wait()

    spread = lax.div(lax.broadcasted_iota(jnp.int32, (nodes, rows), 1), part)
    spread = spread == lax.broadcasted_iota(jnp.int32, (nodes, rows), 0)
    spread = jnp.where(spread, 1.0, 0.0).astype(jnp.bfloat16)
    names = parents[...].astype(jnp.float32).astype(jnp.bfloat16)
    over = (((0,), (1,)), ((), ()))
    across = mm(names, spread).astype(jnp.int32)
    along = lax.dot_general(spread, names, over, preferred_element_type=jnp.float32).astype(jnp.int32)
    place_r = lax.broadcasted_iota(jnp.int32, (rows, rows), 0)
    place_c = lax.broadcasted_iota(jnp.int32, (rows, rows), 1)
    same = lax.rem(place_r, part) == lax.rem(place_c, part)
    for l in range(levels - 1):
        hit = same & (lax.div(place_r, part) == across[l : l + 1, :])
        parent_map[l] = jnp.where(hit, 1.0, 0.0).astype(jnp.bfloat16)
        hit = same & (lax.div(place_c, part) == along[:, l : l + 1])
        child_map[l] = jnp.where(hit, 1.0, 0.0).astype(jnp.bfloat16)

    for fetch in fetches[1:4]:
        fetch.wait()
    ask(0, pair(1))
    ask(1, pair(3))
    last_step = product(halves(to_parent[0, levels - 2]), inverses[0, levels - 2])
    six[...] = halves(last_step)
    root_out[...] = last_step.reshape(nodes, part, rows)
    pl.semaphore_wait(barrier, others)
    ask_up[0].start()
    ask_up[1].start()
    root_up.start()
    for fetch in fetches[4:6]:
        fetch.wait()

    dof = jnp.concatenate([gluing[i : i + 1, :] for i in range(gluing.shape[0])], axis=1)
    sign = jnp.concatenate([signs[i : i + 1, :] for i in range(signs.shape[0])], axis=1)
    coeff = (2 * sign - 1).astype(jnp.float32)
    span = levels * rows
    node = lax.div(dof, span)
    row = lax.rem(dof, span)
    order = lax.broadcasted_iota(jnp.int32, (1, count), 1)
    key = (dof * count + order).astype(jnp.float32)
    first_key = (node * (span * count)).astype(jnp.float32)
    rank = jnp.zeros((1, count), jnp.float32)
    for i in range(count // 128):
        lanes = jnp.broadcast_to(key[:, i * 128 : (i + 1) * 128], (128, 128))
        down_key = jnp.transpose(lanes)
        down_key = jnp.concatenate([down_key] * (count // 128), axis=1)
        before = (down_key < key) & (down_key >= first_key)
        rank = rank + jnp.sum(jnp.where(before, 1.0, 0.0), axis=0, keepdims=True)
    place = rank.astype(jnp.int32) + 1
    fine = place < jnp.where(row < 2 * rows, EARLY, EARLY + LATE)
    overflow = jnp.max(jnp.where(fine, 0.0, 1.0))

    owned = lax.broadcasted_iota(jnp.int32, (nodes, count), 0) == node
    low_part = jnp.where(owned, lax.rem(row, rows).astype(jnp.float32), 0.0).astype(jnp.bfloat16)
    high_part = jnp.where(owned, (lax.div(row, rows) * rows).astype(jnp.float32), 0.0).astype(jnp.bfloat16)
    lane_of = lax.broadcasted_iota(jnp.int32, (columns, count), 0) == place
    lane_of = jnp.where(lane_of, 1.0, 0.0).astype(jnp.bfloat16)
    contract = (((1,), (1,)), ((), ()))
    header = lax.dot_general(low_part, lane_of, contract, preferred_element_type=jnp.float32)
    header = header + lax.dot_general(high_part, lane_of, contract, preferred_element_type=jnp.float32)
    lane = lax.broadcasted_iota(jnp.int32, header.shape, 1)
    header = jnp.where(lane == 0, -1.0, jnp.where(lane < EARLY + LATE, header, overflow))

    fetches[6].wait()
    m_high, m_low = split(multipliers[...])

    def packed(first, size):
        index = lax.broadcasted_iota(jnp.int32, (nodes * size, count), 0)
        inside = (place >= first) & (place < first + size)
        table = jnp.where(index == jnp.where(inside, node * size + place - first, -1), coeff, 0.0).astype(jnp.bfloat16)
        return (mm(table, m_high) + mm(table, m_low)).reshape(nodes, size, columns)

    bucket[...] = packed(0, EARLY)
    for n in range(nodes):
        bucket[n, 0:1, :] = header[n : n + 1, :]
    pack.start()
    late_bucket[...] = packed(EARLY, LATE)

    own[0] = pair(0)

    @pl.loop(0, levels)
    def _(l):
        inverse[l] = halves(inverses[0, l])

    def chain(a, b):
        return mm(a, b).astype(jnp.bfloat16)

    for r in range(rounds):
        w0, w1, w2 = parent_map[2 * r], parent_map[2 * r + 1], parent_map[2 * r + 2]
        near_map[r] = jnp.concatenate([w1, chain(w1, w0)], axis=1)
        both = chain(w2, w1)
        far_map[r] = jnp.concatenate([both, chain(both, w0), w2], axis=1)

    def gather(table, values):
        high, low = split(values)
        return mm(table, high) + mm(table, low)

    def answer(r):
        ask_up[r].arrived()
        found = gather(child_map[2 * r], item_in[2 * rounds + r].reshape(rows, columns))
        item_out[3 * rounds + r] = found.reshape(blocks)
        ask_down[r].start()

    def compose(r):
        ask_down[r].arrived()
        found = item_in[3 * rounds + r].reshape(rows, columns)
        found = jnp.concatenate([found[:, :rows], found[:, rows:]], axis=0)
        step = own[r, :rows]
        leap = own[r, rows:]
        made = product(halves(found), step)
        remote = -made[rows:]
        if r == rounds - 1:
            beyond = item_in[4 * rounds + 1].reshape(rows, columns)[:, rows:]
            remote = remote - product(halves(beyond), leap)
        far[r] = halves(jnp.concatenate([leap - made[:rows], remote, step], axis=0))

    answer(0)
    late_pack.start()

    width = nodes * EARLY

    def glue(level, wanted, source):
        table = lax.broadcasted_iota(jnp.int32, (rows, wanted.shape[1]), 0) + level * rows == wanted
        table = jnp.where(table, 1.0, 0.0).astype(jnp.bfloat16)
        return mm(table, source[0]) + mm(table, source[1])

    fetches[7].wait()
    pack.arrived()
    head = jnp.concatenate([received[n, 0:1, :] for n in range(nodes)], axis=0)
    flag[0, 0] = jnp.where(jnp.max(head[:, EARLY + LATE :]) > 0.0, 1, 0)

    def wide(first, size):
        lanes = lax.broadcasted_iota(jnp.int32, (columns, nodes * size), 1)
        pick = lax.rem(lanes, size) + first == lax.broadcasted_iota(jnp.int32, (columns, nodes * size), 0)
        pick = jnp.where(pick, 1.0, 0.0).astype(jnp.bfloat16)
        high, low = split(head)
        found = mm(high, pick) + mm(low, pick)
        sender = lax.div(lax.broadcasted_iota(jnp.int32, found.shape, 1), size)
        mine = sender == lax.broadcasted_iota(jnp.int32, found.shape, 0)
        return jnp.sum(jnp.where(mine, found, 0.0), axis=0, keepdims=True).astype(jnp.int32)

    early_rows = wide(0, EARLY)
    high, low = split(received[...].reshape(width, columns))
    rows_high[:width], rows_low[:width] = high, low
    for l in range(2):
        pending[l] = loads[0, l] - glue(l, early_rows, (high, low))

    def solve(level, x):
        out[0, level] = product(inverse[level], x)

    def skipped(r):
        step_down[r].arrived()
        solve(2 * r + 1, pending[2 * r + 1] - item_in[rounds + r].reshape(rows, columns))

    for r in range(rounds):
        level = 2 * r
        if r > 0:
            down[2 * r - 1].arrived()
            pending[level + 1] = pending[level + 1] - down_in[2 * r - 1].reshape(rows, columns)
        e = product(near[r], pending[level + 1])
        up_out[r, :, 0:part] = e[:rows].reshape(blocks)
        up_out[r, :, part : 2 * part] = e[rows:].reshape(blocks)
        up[r].start_piece(0)
        if r == 0:
            compose(0)
        else:
            down[2 * r - 2].arrived()
            pending[level] = pending[level] - down_in[2 * r - 2].reshape(rows, columns)
        c = product(far[r, : 2 * rows], pending[level])
        up_out[r, :, 2 * part : 3 * part] = c[:rows].reshape(blocks)
        up_out[r, :, 3 * part :] = c[rows:].reshape(blocks)
        up[r].start_piece(2 * part)
        item_out[r] = product(far[r, 2 * rows :], pending[level]).reshape(blocks)
        step_up[r].start()
        solve(level, pending[level])

        if r == 0:
            step_five[...] = pair(5)
            for later in range(1, rounds):
                own[later] = pair(2 * later)
            answer(1)
            late_pack.arrived()
            every_row = jnp.concatenate([early_rows, wide(EARLY, LATE)], axis=1)
            rows_high[width:], rows_low[width:] = split(late_received[...].reshape(nodes * LATE, columns))

            @pl.loop(2, levels)
            def _(l):
                pending[l] = loads[0, l] - glue(l, every_row, (rows_high[...], rows_low[...]))

            root_up.arrived()
            six_in = root_in[...].reshape(rows, rows)
            above = gather(child_map[5], six_in)
            above = jnp.concatenate([above, gather(child_map[4], above)], axis=1)
            item_out[4 * rounds + 1] = above.reshape(blocks)
            root_down.start()
            item_out[4 * rounds] = product(six[...], pending[levels - 2]).reshape(blocks)
        else:
            skipped(r - 1)
        if r == 1:
            answer(2)

        up[r].arrived()
        second = jnp.concatenate([up_in[r, :, i * part : (i + 1) * part].reshape(rows, columns) for i in (1, 3)], axis=0)
        if r == rounds - 1:
            tail_up.arrived()
            second = jnp.concatenate([second, item_in[4 * rounds].reshape(rows, columns)], axis=0)
            second = gather(far_map[r], second)
        else:
            second = gather(far_map[r, :, : 2 * rows], second)
        down_out[2 * r + 1] = second.reshape(blocks)
        down[2 * r + 1].start()
        first = jnp.concatenate([up_in[r, :, i * part : (i + 1) * part].reshape(rows, columns) for i in (0, 2)], axis=0)
        down_out[2 * r] = gather(near_map[r], first).reshape(blocks)
        down[2 * r].start()
        if r == 1:
            tail_up.start()
        step_up[r].arrived()
        item_out[rounds + r] = gather(parent_map[level], item_in[r].reshape(rows, columns)).reshape(blocks)
        step_down[r].start()

        if r == 0:
            root_down.arrived()
            beyond = item_in[4 * rounds + 1].reshape(rows, columns)[:, :rows]
            five = step_five[...]
            ask(2, jnp.concatenate([five[:rows], five[rows:] - product(halves(beyond), five[:rows])], axis=0))
            ask_up[2].start()
        if r < rounds - 1:
            compose(r + 1)

    down[2 * rounds - 1].arrived()
    solve(levels - 1, pending[levels - 1] - down_in[2 * rounds - 1].reshape(rows, columns))
    down[2 * rounds - 2].arrived()
    solve(levels - 2, pending[levels - 2] - down_in[2 * rounds - 2].reshape(rows, columns))
    skipped(rounds - 1)

    for exchange in everything:
        exchange.sent()


def direct(loads, multipliers, gluing, signs, parents, inverses, to_parent, grandparent_factor):
    nodes = parents.shape[0]
    _, levels, rows, columns = loads.shape
    count = multipliers.shape[0]
    f32, bf16 = jnp.float32, jnp.bfloat16
    rounds = levels // 2 - 1
    part = rows // nodes
    items = 4 * rounds + 2
    dma = pltpu.SemaphoreType.DMA
    vmem = pl.BlockSpec(memory_space=pltpu.VMEM)
    return pl.pallas_call(
        kernel,
        out_shape=(
            jax.ShapeDtypeStruct(loads.shape, f32),
            jax.ShapeDtypeStruct((1, 1), jnp.int32),
        ),
        in_specs=[pl.BlockSpec(memory_space=pltpu.HBM)] * 8,
        out_specs=(vmem, pl.BlockSpec(memory_space=pltpu.SMEM)),
        scratch_shapes=[
            pltpu.VMEM(loads.shape, f32),
            pltpu.VMEM(multipliers.shape, f32),
            pltpu.VMEM((count // 128, 128), jnp.int32),
            pltpu.VMEM((count // 128, 128), jnp.int32),
            pltpu.VMEM((levels - 1, nodes), jnp.int32),
            pltpu.VMEM(inverses.shape, f32),
            pltpu.VMEM(to_parent.shape, f32),
            pltpu.VMEM(grandparent_factor.shape, f32),
            dma((8,)),
            pltpu.VMEM((nodes, EARLY, columns), f32),
            pltpu.VMEM((nodes, EARLY, columns), f32),
            pltpu.VMEM((nodes, LATE, columns), f32),
            pltpu.VMEM((nodes, LATE, columns), f32),
            pltpu.VMEM((nodes * (EARLY + LATE), columns), bf16),
            pltpu.VMEM((nodes * (EARLY + LATE), columns), bf16),
            pltpu.VMEM((levels, rows, columns), f32),
            pltpu.VMEM((levels - 1, rows, rows), bf16),
            pltpu.VMEM((levels - 1, rows, rows), bf16),
            pltpu.VMEM((rounds, rows, 2 * rows), bf16),
            pltpu.VMEM((rounds, rows, 3 * rows), bf16),
            pltpu.VMEM((levels, rows, 2 * rows), bf16),
            pltpu.VMEM((rounds, 2 * rows, 2 * rows), bf16),
            pltpu.VMEM((rounds, 3 * rows, 2 * rows), bf16),
            pltpu.VMEM((rows, 2 * rows), bf16),
            pltpu.VMEM((2 * rows, rows), f32),
            pltpu.VMEM((rounds, 2 * rows, rows), f32),
            pltpu.VMEM((rounds, nodes, 4 * part, columns), f32),
            pltpu.VMEM((rounds, nodes, 4 * part, columns), f32),
            pltpu.VMEM((2 * rounds, nodes, part, columns), f32),
            pltpu.VMEM((2 * rounds, nodes, part, columns), f32),
            pltpu.VMEM((items, nodes, part, columns), f32),
            pltpu.VMEM((items, nodes, part, columns), f32),
            pltpu.VMEM((nodes, part, rows), f32),
            pltpu.VMEM((nodes, part, rows), f32),
            dma((2,)),
            dma((2,)),
            dma((rounds,)),
            dma((rounds,)),
            dma((2 * rounds,)),
            dma((2 * rounds,)),
            dma((items,)),
            dma((items,)),
            dma((1,)),
            dma((1,)),
        ],
        compiler_params=pltpu.CompilerParams(
            collective_id=0, has_side_effects=True, vmem_limit_bytes=48 * 1024 * 1024
        ),
    )(
        loads,
        multipliers,
        gluing.reshape(count // 128, 128),
        signs.reshape(count // 128, 128),
        parents.T,
        inverses,
        to_parent,
        grandparent_factor,
    )


def general(loads, multipliers, gluing, signs, parents, inverses, to_parent, grandparent_factor):
    me = lax.axis_index("group")
    size = lax.axis_size("group")
    levels, rows, columns = loads.shape[1:]
    span = levels * rows
    ring = [(i, (i + 1) % size) for i in range(size)]
    exact = lax.Precision.HIGHEST

    def passed(value):
        return lax.ppermute(value, "group", ring)

    target = (me * span + lax.iota(jnp.int32, span)).astype(jnp.float32)

    def add(_, state):
        glued, values, at = state
        table = jnp.where(target[:, None] == at[None, :], 1.0, 0.0)
        glued = glued + jnp.dot(table, values, precision=exact)
        return glued, passed(values), passed(at)

    coeff = (2 * signs - 1).astype(jnp.float32)
    start = (jnp.zeros((span, columns), jnp.float32), coeff[:, None] * multipliers, gluing.astype(jnp.float32))
    glued = lax.fori_loop(0, size, add, start)[0]
    pending = loads[0] - glued.reshape(levels, rows, columns)
    pending = jnp.concatenate([pending, jnp.zeros((2, rows, columns), jnp.float32)])
    one = jnp.concatenate([to_parent[0], jnp.zeros((1, rows, rows), jnp.float32)])
    two = jnp.concatenate([grandparent_factor[0], jnp.zeros((2, rows, rows), jnp.float32)])
    firsts = jnp.concatenate([parents, jnp.zeros((size, 2), jnp.int32)], axis=1)

    def level(l, state):
        pending, solved = state
        x = jnp.dot(inverses[0, l], pending[l], precision=exact)
        solved = solved.at[l].set(x)
        first = firsts[:, l]
        second = firsts[first, l + 1]

        def take(s, state):
            here, there, up, leap = state
            source = lax.rem(me - s + size, size)
            here = here + jnp.where(first[source] == me, up, 0.0)
            there = there + jnp.where(second[source] == me, leap, 0.0)
            return here, there, passed(up), passed(leap)

        zero = jnp.zeros((rows, columns), jnp.float32)
        up = jnp.dot(one[l], x, precision=exact)
        leap = jnp.dot(two[l], x, precision=exact)
        here, there, _, _ = lax.fori_loop(0, size, take, (zero, zero, up, leap))
        return pending.at[l + 1].add(-here).at[l + 2].add(-there), solved

    solved = lax.fori_loop(0, levels, level, (pending, jnp.zeros(loads.shape[1:], jnp.float32)))[1]
    return solved[None]


def finish_kernel(source, target, done):
    pieces = [pltpu.make_async_copy(source.at[0, l], target.at[0, l], done.at[l]) for l in range(source.shape[1])]
    for piece in pieces:
        piece.start()
    for piece in pieces:
        piece.wait()


def finish(solved):
    return pl.pallas_call(
        finish_kernel,
        out_shape=jax.ShapeDtypeStruct(solved.shape, solved.dtype),
        in_specs=[pl.BlockSpec(memory_space=pltpu.VMEM)],
        out_specs=pl.BlockSpec(memory_space=pl.ANY),
        scratch_shapes=[pltpu.SemaphoreType.DMA((solved.shape[1],))],
    )(solved)


def body(*args):
    solved, flag = direct(*args)
    return lax.switch(flag[0, 0], (lambda: finish(solved), lambda: general(*args)))


def solution(mesh):
    return jax.shard_map(
        body,
        mesh=mesh,
        in_specs=(
            P(("cluster", "group"), None, None, None),
            P(("cluster", "group"), None),
            P(("cluster", "group")),
            P(("cluster", "group")),
            P("cluster", None),
            P(("cluster", "group"), None, None, None),
            P(("cluster", "group"), None, None, None),
            P(("cluster", "group"), None, None, None),
        ),
        out_specs=P(("cluster", "group"), None, None, None),
        check_vma=False,
    )
```

```python
import jax
import jax.numpy as jnp
from jax import lax
from jax.experimental import pallas as pl
from jax.experimental.pallas import tpu as pltpu
from jax.sharding import PartitionSpec as P

EARLY = 32
LATE = 32
PIECE = 16


def split(x):
    high = x.astype(jnp.bfloat16)
    return high, (x - high.astype(jnp.float32)).astype(jnp.bfloat16)


def mm(a, b):
    return jnp.dot(a, b, preferred_element_type=jnp.float32)


def halves(matrix):
    return jnp.concatenate(split(matrix), axis=1)


def product(matrix, x):
    high, low = split(x)
    return mm(matrix, jnp.concatenate([high, high], axis=0)) + mm(matrix[:, : matrix.shape[1] // 2], low)


def kernel(
    loads_hbm, multipliers_hbm, gluing_hbm, signs_hbm, parents_hbm, inverses_hbm, to_parent_hbm, grandparent_hbm,
    out, flag,
    loads, multipliers, gluing, signs, parents, inverses, to_parent, grandparent, fetched,
    bucket, received, late_bucket, late_received, rows_high, rows_low, pending, parent_map, child_map, near_map, far_map,
    inverse, near, far, six, step_five, own,
    up_out, up_in, down_out, down_in, item_out, item_in, root_out, root_in,
    pack_send, pack_recv, up_send, up_recv, down_send, down_recv, item_send, item_recv, root_send, root_recv,
):
    nodes = parents.shape[1]
    levels, rows, columns = loads.shape[1:]
    count = multipliers.shape[0]
    me = lax.axis_index("group")
    others = nodes - 1
    part = rows // nodes
    rounds = levels // 2 - 1
    blocks = (nodes, part, columns)

    arguments = (
        (parents_hbm, parents),
        (to_parent_hbm, to_parent),
        (grandparent_hbm, grandparent),
        (inverses_hbm, inverses),
        (gluing_hbm, gluing),
        (signs_hbm, signs),
        (multipliers_hbm, multipliers),
        (loads_hbm, loads),
    )
    fetches = [pltpu.make_async_copy(far, near, fetched.at[i]) for i, (far, near) in enumerate(arguments)]
    apart = [(2, 2), (2, 3), (3, 2), (2, 1), (1, 2), (3, 3), (1, 1), (3, 1), (1, 3), (0, 2), (2, 0), (0, 1), (1, 0), (0, 3), (3, 0)]
    peers = [4 * lax.rem(lax.div(me, 4) + y, 4) + lax.rem(lax.rem(me, 4) + x, 4) for y, x in apart]

    def copy(source, target, send, recv, device):
        return pltpu.make_async_remote_copy(
            src_ref=source,
            dst_ref=target,
            send_sem=send,
            recv_sem=recv,
            device_id={"group": device},
            device_id_type=pl.DeviceIdType.MESH,
        )

    class Exchange:
        def __init__(self, source, target, send, recv):
            self.source, self.target, self.send, self.recv = source, target, send, recv

        def start(self):
            for first in range(0, self.source.shape[1], PIECE):
                self.start_piece(first)

        def start_piece(self, first):
            size = min(PIECE, self.source.shape[1])
            here = pl.ds(first, size)
            for device in peers:
                copy(self.source.at[device, here], self.target.at[me, here], self.send, self.recv, device).start()
            self.target[me, first : first + size] = self.source[me, first : first + size]

        def all(self):
            most = pl.ds(0, others)
            return copy(self.source.at[most], self.target.at[most], self.send, self.recv, peers[0])

        def arrived(self):
            self.all().wait_recv()

        def sent(self):
            self.all().wait_send()

    def item(i):
        return Exchange(item_out.at[i], item_in.at[i], item_send.at[i], item_recv.at[i])

    pack = Exchange(bucket, received, pack_send.at[0], pack_recv.at[0])
    late_pack = Exchange(late_bucket, late_received, pack_send.at[1], pack_recv.at[1])
    up = [Exchange(up_out.at[r], up_in.at[r], up_send.at[r], up_recv.at[r]) for r in range(rounds)]
    down = [Exchange(down_out.at[r], down_in.at[r], down_send.at[r], down_recv.at[r]) for r in range(2 * rounds)]
    step_up = [item(r) for r in range(rounds)]
    step_down = [item(rounds + r) for r in range(rounds)]
    ask_up = [item(2 * rounds + r) for r in range(rounds)]
    ask_down = [item(3 * rounds + r) for r in range(rounds)]
    tail_up = item(4 * rounds)
    root_down = item(4 * rounds + 1)
    root_up = Exchange(root_out, root_in, root_send.at[0], root_recv.at[0])
    everything = [pack, late_pack, *up, *down, *step_up, *step_down, *ask_up, *ask_down, tail_up, root_down, root_up]

    barrier = pltpu.get_barrier_semaphore()
    for device in peers:
        pl.semaphore_signal(barrier, inc=1, device_id={"group": device}, device_id_type=pl.DeviceIdType.MESH)
    for fetch in fetches:
        fetch.start()

    def pair(level):
        both = jnp.concatenate([to_parent[0, level], grandparent[0, level]], axis=0)
        return product(halves(both), inverses[0, level])

    def ask(r, both):
        near[r] = halves(both)
        item_out[2 * rounds + r] = jnp.concatenate([both[:rows], both[rows:]], axis=1).reshape(blocks)

    fetches[0].wait()

    spread = lax.div(lax.broadcasted_iota(jnp.int32, (nodes, rows), 1), part)
    spread = spread == lax.broadcasted_iota(jnp.int32, (nodes, rows), 0)
    spread = jnp.where(spread, 1.0, 0.0).astype(jnp.bfloat16)
    names = parents[...].astype(jnp.float32).astype(jnp.bfloat16)
    over = (((0,), (1,)), ((), ()))
    across = mm(names, spread).astype(jnp.int32)
    along = lax.dot_general(spread, names, over, preferred_element_type=jnp.float32).astype(jnp.int32)
    place_r = lax.broadcasted_iota(jnp.int32, (rows, rows), 0)
    place_c = lax.broadcasted_iota(jnp.int32, (rows, rows), 1)
    same = lax.rem(place_r, part) == lax.rem(place_c, part)
    for l in range(levels - 1):
        hit = same & (lax.div(place_r, part) == across[l : l + 1, :])
        parent_map[l] = jnp.where(hit, 1.0, 0.0).astype(jnp.bfloat16)
        hit = same & (lax.div(place_c, part) == along[:, l : l + 1])
        child_map[l] = jnp.where(hit, 1.0, 0.0).astype(jnp.bfloat16)

    for fetch in fetches[1:4]:
        fetch.wait()
    ask(0, pair(1))
    ask(1, pair(3))
    last_step = product(halves(to_parent[0, levels - 2]), inverses[0, levels - 2])
    six[...] = halves(last_step)
    root_out[...] = last_step.reshape(nodes, part, rows)
    pl.semaphore_wait(barrier, others)
    ask_up[0].start()
    ask_up[1].start()
    root_up.start()
    for fetch in fetches[4:6]:
        fetch.wait()

    dof = jnp.concatenate([gluing[i : i + 1, :] for i in range(gluing.shape[0])], axis=1)
    sign = jnp.concatenate([signs[i : i + 1, :] for i in range(signs.shape[0])], axis=1)
    coeff = (2 * sign - 1).astype(jnp.float32)
    span = levels * rows
    node = lax.div(dof, span)
    row = lax.rem(dof, span)
    order = lax.broadcasted_iota(jnp.int32, (1, count), 1)
    key = (dof * count + order).astype(jnp.float32)
    first_key = (node * (span * count)).astype(jnp.float32)
    rank = jnp.zeros((1, count), jnp.float32)
    for i in range(count // 128):
        lanes = jnp.broadcast_to(key[:, i * 128 : (i + 1) * 128], (128, 128))
        down_key = jnp.transpose(lanes)
        down_key = jnp.concatenate([down_key] * (count // 128), axis=1)
        before = (down_key < key) & (down_key >= first_key)
        rank = rank + jnp.sum(jnp.where(before, 1.0, 0.0), axis=0, keepdims=True)
    place = rank.astype(jnp.int32) + 1
    fine = place < jnp.where(row < 2 * rows, EARLY, EARLY + LATE)
    overflow = jnp.max(jnp.where(fine, 0.0, 1.0))

    owned = lax.broadcasted_iota(jnp.int32, (nodes, count), 0) == node
    low_part = jnp.where(owned, lax.rem(row, rows).astype(jnp.float32), 0.0).astype(jnp.bfloat16)
    high_part = jnp.where(owned, (lax.div(row, rows) * rows).astype(jnp.float32), 0.0).astype(jnp.bfloat16)
    lane_of = lax.broadcasted_iota(jnp.int32, (columns, count), 0) == place
    lane_of = jnp.where(lane_of, 1.0, 0.0).astype(jnp.bfloat16)
    contract = (((1,), (1,)), ((), ()))
    header = lax.dot_general(low_part, lane_of, contract, preferred_element_type=jnp.float32)
    header = header + lax.dot_general(high_part, lane_of, contract, preferred_element_type=jnp.float32)
    lane = lax.broadcasted_iota(jnp.int32, header.shape, 1)
    header = jnp.where(lane == 0, -1.0, jnp.where(lane < EARLY + LATE, header, overflow))

    fetches[6].wait()
    m_high, m_low = split(multipliers[...])

    def packed(first, size):
        index = lax.broadcasted_iota(jnp.int32, (nodes * size, count), 0)
        inside = (place >= first) & (place < first + size)
        table = jnp.where(index == jnp.where(inside, node * size + place - first, -1), coeff, 0.0).astype(jnp.bfloat16)
        return (mm(table, m_high) + mm(table, m_low)).reshape(nodes, size, columns)

    bucket[...] = packed(0, EARLY)
    for n in range(nodes):
        bucket[n, 0:1, :] = header[n : n + 1, :]
    pack.start()
    late_bucket[...] = packed(EARLY, LATE)

    own[0] = pair(0)

    @pl.loop(0, levels)
    def _(l):
        inverse[l] = halves(inverses[0, l])

    def chain(a, b):
        return mm(a, b).astype(jnp.bfloat16)

    for r in range(rounds):
        w0, w1, w2 = parent_map[2 * r], parent_map[2 * r + 1], parent_map[2 * r + 2]
        near_map[r] = jnp.concatenate([w1, chain(w1, w0)], axis=1)
        both = chain(w2, w1)
        far_map[r] = jnp.concatenate([both, chain(both, w0), w2], axis=1)

    def gather(table, values):
        high, low = split(values)
        return mm(table, high) + mm(table, low)

    def answer(r):
        ask_up[r].arrived()
        found = gather(child_map[2 * r], item_in[2 * rounds + r].reshape(rows, columns))
        item_out[3 * rounds + r] = found.reshape(blocks)
        ask_down[r].start()

    def compose(r):
        ask_down[r].arrived()
        found = item_in[3 * rounds + r].reshape(rows, columns)
        found = jnp.concatenate([found[:, :rows], found[:, rows:]], axis=0)
        step = own[r, :rows]
        leap = own[r, rows:]
        made = product(halves(found), step)
        remote = -made[rows:]
        if r == rounds - 1:
            beyond = item_in[4 * rounds + 1].reshape(rows, columns)[:, rows:]
            remote = remote - product(halves(beyond), leap)
        far[r] = halves(jnp.concatenate([leap - made[:rows], remote, step], axis=0))

    answer(0)
    late_pack.start()

    width = nodes * EARLY

    def glue(level, wanted, source):
        table = lax.broadcasted_iota(jnp.int32, (rows, wanted.shape[1]), 0) + level * rows == wanted
        table = jnp.where(table, 1.0, 0.0).astype(jnp.bfloat16)
        return mm(table, source[0]) + mm(table, source[1])

    fetches[7].wait()
    pack.arrived()
    head = jnp.concatenate([received[n, 0:1, :] for n in range(nodes)], axis=0)
    flag[0, 0] = jnp.where(jnp.max(head[:, EARLY + LATE :]) > 0.0, 1, 0)

    def wide(first, size):
        lanes = lax.broadcasted_iota(jnp.int32, (columns, nodes * size), 1)
        pick = lax.rem(lanes, size) + first == lax.broadcasted_iota(jnp.int32, (columns, nodes * size), 0)
        pick = jnp.where(pick, 1.0, 0.0).astype(jnp.bfloat16)
        high, low = split(head)
        found = mm(high, pick) + mm(low, pick)
        sender = lax.div(lax.broadcasted_iota(jnp.int32, found.shape, 1), size)
        mine = sender == lax.broadcasted_iota(jnp.int32, found.shape, 0)
        return jnp.sum(jnp.where(mine, found, 0.0), axis=0, keepdims=True).astype(jnp.int32)

    early_rows = wide(0, EARLY)
    high, low = split(received[...].reshape(width, columns))
    rows_high[:width], rows_low[:width] = high, low
    for l in range(2):
        pending[l] = loads[0, l] - glue(l, early_rows, (high, low))

    def solve(level, x):
        out[0, level] = product(inverse[level], x)

    def skipped(r):
        step_down[r].arrived()
        solve(2 * r + 1, pending[2 * r + 1] - item_in[rounds + r].reshape(rows, columns))

    for r in range(rounds):
        level = 2 * r
        if r > 0:
            down[2 * r - 1].arrived()
            pending[level + 1] = pending[level + 1] - down_in[2 * r - 1].reshape(rows, columns)
        e = product(near[r], pending[level + 1])
        up_out[r, :, 0:part] = e[:rows].reshape(blocks)
        up_out[r, :, part : 2 * part] = e[rows:].reshape(blocks)
        up[r].start_piece(0)
        if r == 0:
            compose(0)
        else:
            down[2 * r - 2].arrived()
            pending[level] = pending[level] - down_in[2 * r - 2].reshape(rows, columns)
        c = product(far[r, : 2 * rows], pending[level])
        up_out[r, :, 2 * part : 3 * part] = c[:rows].reshape(blocks)
        up_out[r, :, 3 * part :] = c[rows:].reshape(blocks)
        up[r].start_piece(2 * part)
        item_out[r] = product(far[r, 2 * rows :], pending[level]).reshape(blocks)
        step_up[r].start()
        solve(level, pending[level])

        if r == 0:
            step_five[...] = pair(5)
            for later in range(1, rounds):
                own[later] = pair(2 * later)
            answer(1)
            late_pack.arrived()
            every_row = jnp.concatenate([early_rows, wide(EARLY, LATE)], axis=1)
            rows_high[width:], rows_low[width:] = split(late_received[...].reshape(nodes * LATE, columns))

            @pl.loop(2, levels)
            def _(l):
                pending[l] = loads[0, l] - glue(l, every_row, (rows_high[...], rows_low[...]))

            root_up.arrived()
            six_in = root_in[...].reshape(rows, rows)
            above = gather(child_map[5], six_in)
            above = jnp.concatenate([above, gather(child_map[4], above)], axis=1)
            item_out[4 * rounds + 1] = above.reshape(blocks)
            root_down.start()
            item_out[4 * rounds] = product(six[...], pending[levels - 2]).reshape(blocks)
        else:
            skipped(r - 1)
        if r == 1:
            answer(2)

        up[r].arrived()
        second = jnp.concatenate([up_in[r, :, i * part : (i + 1) * part].reshape(rows, columns) for i in (1, 3)], axis=0)
        if r == rounds - 1:
            tail_up.arrived()
            second = jnp.concatenate([second, item_in[4 * rounds].reshape(rows, columns)], axis=0)
            second = gather(far_map[r], second)
        else:
            second = gather(far_map[r, :, : 2 * rows], second)
        down_out[2 * r + 1] = second.reshape(blocks)
        down[2 * r + 1].start()
        first = jnp.concatenate([up_in[r, :, i * part : (i + 1) * part].reshape(rows, columns) for i in (0, 2)], axis=0)
        down_out[2 * r] = gather(near_map[r], first).reshape(blocks)
        down[2 * r].start()
        if r == 1:
            tail_up.start()
        step_up[r].arrived()
        item_out[rounds + r] = gather(parent_map[level], item_in[r].reshape(rows, columns)).reshape(blocks)
        step_down[r].start()

        if r == 0:
            root_down.arrived()
            beyond = item_in[4 * rounds + 1].reshape(rows, columns)[:, :rows]
            five = step_five[...]
            ask(2, jnp.concatenate([five[:rows], five[rows:] - product(halves(beyond), five[:rows])], axis=0))
            ask_up[2].start()
        if r < rounds - 1:
            compose(r + 1)

    down[2 * rounds - 1].arrived()
    solve(levels - 1, pending[levels - 1] - down_in[2 * rounds - 1].reshape(rows, columns))
    down[2 * rounds - 2].arrived()
    solve(levels - 2, pending[levels - 2] - down_in[2 * rounds - 2].reshape(rows, columns))
    skipped(rounds - 1)

    for exchange in everything:
        exchange.sent()


def direct(loads, multipliers, gluing, signs, parents, inverses, to_parent, grandparent_factor):
    nodes = parents.shape[0]
    _, levels, rows, columns = loads.shape
    count = multipliers.shape[0]
    f32, bf16 = jnp.float32, jnp.bfloat16
    rounds = levels // 2 - 1
    part = rows // nodes
    items = 4 * rounds + 2
    dma = pltpu.SemaphoreType.DMA
    vmem = pl.BlockSpec(memory_space=pltpu.VMEM)
    return pl.pallas_call(
        kernel,
        out_shape=(
            jax.ShapeDtypeStruct(loads.shape, f32),
            jax.ShapeDtypeStruct((1, 1), jnp.int32),
        ),
        in_specs=[pl.BlockSpec(memory_space=pltpu.HBM)] * 8,
        out_specs=(vmem, pl.BlockSpec(memory_space=pltpu.SMEM)),
        scratch_shapes=[
            pltpu.VMEM(loads.shape, f32),
            pltpu.VMEM(multipliers.shape, f32),
            pltpu.VMEM((count // 128, 128), jnp.int32),
            pltpu.VMEM((count // 128, 128), jnp.int32),
            pltpu.VMEM((levels - 1, nodes), jnp.int32),
            pltpu.VMEM(inverses.shape, f32),
            pltpu.VMEM(to_parent.shape, f32),
            pltpu.VMEM(grandparent_factor.shape, f32),
            dma((8,)),
            pltpu.VMEM((nodes, EARLY, columns), f32),
            pltpu.VMEM((nodes, EARLY, columns), f32),
            pltpu.VMEM((nodes, LATE, columns), f32),
            pltpu.VMEM((nodes, LATE, columns), f32),
            pltpu.VMEM((nodes * (EARLY + LATE), columns), bf16),
            pltpu.VMEM((nodes * (EARLY + LATE), columns), bf16),
            pltpu.VMEM((levels, rows, columns), f32),
            pltpu.VMEM((levels - 1, rows, rows), bf16),
            pltpu.VMEM((levels - 1, rows, rows), bf16),
            pltpu.VMEM((rounds, rows, 2 * rows), bf16),
            pltpu.VMEM((rounds, rows, 3 * rows), bf16),
            pltpu.VMEM((levels, rows, 2 * rows), bf16),
            pltpu.VMEM((rounds, 2 * rows, 2 * rows), bf16),
            pltpu.VMEM((rounds, 3 * rows, 2 * rows), bf16),
            pltpu.VMEM((rows, 2 * rows), bf16),
            pltpu.VMEM((2 * rows, rows), f32),
            pltpu.VMEM((rounds, 2 * rows, rows), f32),
            pltpu.VMEM((rounds, nodes, 4 * part, columns), f32),
            pltpu.VMEM((rounds, nodes, 4 * part, columns), f32),
            pltpu.VMEM((2 * rounds, nodes, part, columns), f32),
            pltpu.VMEM((2 * rounds, nodes, part, columns), f32),
            pltpu.VMEM((items, nodes, part, columns), f32),
            pltpu.VMEM((items, nodes, part, columns), f32),
            pltpu.VMEM((nodes, part, rows), f32),
            pltpu.VMEM((nodes, part, rows), f32),
            dma((2,)),
            dma((2,)),
            dma((rounds,)),
            dma((rounds,)),
            dma((2 * rounds,)),
            dma((2 * rounds,)),
            dma((items,)),
            dma((items,)),
            dma((1,)),
            dma((1,)),
        ],
        compiler_params=pltpu.CompilerParams(
            collective_id=0, has_side_effects=True, vmem_limit_bytes=48 * 1024 * 1024
        ),
    )(
        loads,
        multipliers,
        gluing.reshape(count // 128, 128),
        signs.reshape(count // 128, 128),
        parents.T,
        inverses,
        to_parent,
        grandparent_factor,
    )


def general(loads, multipliers, gluing, signs, parents, inverses, to_parent, grandparent_factor):
    me = lax.axis_index("group")
    size = lax.axis_size("group")
    levels, rows, columns = loads.shape[1:]
    span = levels * rows
    ring = [(i, (i + 1) % size) for i in range(size)]
    exact = lax.Precision.HIGHEST

    def passed(value):
        return lax.ppermute(value, "group", ring)

    target = (me * span + lax.iota(jnp.int32, span)).astype(jnp.float32)

    def add(_, state):
        glued, values, at = state
        table = jnp.where(target[:, None] == at[None, :], 1.0, 0.0)
        glued = glued + jnp.dot(table, values, precision=exact)
        return glued, passed(values), passed(at)

    coeff = (2 * signs - 1).astype(jnp.float32)
    start = (jnp.zeros((span, columns), jnp.float32), coeff[:, None] * multipliers, gluing.astype(jnp.float32))
    glued = lax.fori_loop(0, size, add, start)[0]
    pending = loads[0] - glued.reshape(levels, rows, columns)
    pending = jnp.concatenate([pending, jnp.zeros((2, rows, columns), jnp.float32)])
    one = jnp.concatenate([to_parent[0], jnp.zeros((1, rows, rows), jnp.float32)])
    two = jnp.concatenate([grandparent_factor[0], jnp.zeros((2, rows, rows), jnp.float32)])
    firsts = jnp.concatenate([parents, jnp.zeros((size, 2), jnp.int32)], axis=1)

    def level(l, state):
        pending, solved = state
        x = jnp.dot(inverses[0, l], pending[l], precision=exact)
        solved = solved.at[l].set(x)
        first = firsts[:, l]
        second = firsts[first, l + 1]

        def take(s, state):
            here, there, up, leap = state
            source = lax.rem(me - s + size, size)
            here = here + jnp.where(first[source] == me, up, 0.0)
            there = there + jnp.where(second[source] == me, leap, 0.0)
            return here, there, passed(up), passed(leap)

        zero = jnp.zeros((rows, columns), jnp.float32)
        up = jnp.dot(one[l], x, precision=exact)
        leap = jnp.dot(two[l], x, precision=exact)
        here, there, _, _ = lax.fori_loop(0, size, take, (zero, zero, up, leap))
        return pending.at[l + 1].add(-here).at[l + 2].add(-there), solved

    solved = lax.fori_loop(0, levels, level, (pending, jnp.zeros(loads.shape[1:], jnp.float32)))[1]
    return solved[None]


def finish_kernel(source, target, done):
    pieces = [pltpu.make_async_copy(source.at[0, l], target.at[0, l], done.at[l]) for l in range(source.shape[1])]
    for piece in pieces:
        piece.start()
    for piece in pieces:
        piece.wait()


def finish(solved):
    return pl.pallas_call(
        finish_kernel,
        out_shape=jax.ShapeDtypeStruct(solved.shape, solved.dtype),
        in_specs=[pl.BlockSpec(memory_space=pltpu.VMEM)],
        out_specs=pl.BlockSpec(memory_space=pl.ANY),
        scratch_shapes=[pltpu.SemaphoreType.DMA((solved.shape[1],))],
    )(solved)


def body(*args):
    solved, flag = direct(*args)
    return lax.switch(flag[0, 0], (lambda: finish(solved), lambda: general(*args)))


def solution(mesh):
    return jax.shard_map(
        body,
        mesh=mesh,
        in_specs=(
            P(("cluster", "group"), None, None, None),
            P(("cluster", "group"), None),
            P(("cluster", "group")),
            P(("cluster", "group")),
            P("cluster", None),
            P(("cluster", "group"), None, None, None),
            P(("cluster", "group"), None, None, None),
            P(("cluster", "group"), None, None, None),
        ),
        out_specs=P(("cluster", "group"), None, None, None),
        check_vma=False,
    )
```

```python
import jax
import jax.numpy as jnp
from jax import lax
from jax.experimental import pallas as pl
from jax.experimental.pallas import tpu as pltpu
from jax.sharding import PartitionSpec as P

EARLY = 32
LATE = 32
PIECE = 16


def split(x):
    high = x.astype(jnp.bfloat16)
    return high, (x - high.astype(jnp.float32)).astype(jnp.bfloat16)


def mm(a, b):
    return jnp.dot(a, b, preferred_element_type=jnp.float32)


def halves(matrix):
    return jnp.concatenate(split(matrix), axis=1)


def product(matrix, x):
    high, low = split(x)
    return mm(matrix, jnp.concatenate([high, high], axis=0)) + mm(matrix[:, : matrix.shape[1] // 2], low)


def kernel(
    loads_hbm, multipliers_hbm, gluing_hbm, signs_hbm, parents_hbm, inverses_hbm, to_parent_hbm, grandparent_hbm,
    out, flag,
    loads, multipliers, gluing, signs, parents, inverses, to_parent, grandparent, fetched,
    bucket, received, late_bucket, late_received, rows_high, rows_low, pending, parent_map, child_map, near_map, far_map,
    inverse, near, far, six, step_five, own,
    up_out, up_in, down_out, down_in, item_out, item_in, root_out, root_in,
    pack_send, pack_recv, up_send, up_recv, down_send, down_recv, item_send, item_recv, root_send, root_recv,
):
    nodes = parents.shape[1]
    levels, rows, columns = loads.shape[1:]
    count = multipliers.shape[0]
    me = lax.axis_index("group")
    others = nodes - 1
    part = rows // nodes
    rounds = levels // 2 - 1
    blocks = (nodes, part, columns)

    arguments = (
        (parents_hbm, parents),
        (to_parent_hbm, to_parent),
        (grandparent_hbm, grandparent),
        (inverses_hbm, inverses),
        (gluing_hbm, gluing),
        (signs_hbm, signs),
        (multipliers_hbm, multipliers),
        (loads_hbm, loads),
    )
    fetches = [pltpu.make_async_copy(far, near, fetched.at[i]) for i, (far, near) in enumerate(arguments)]
    apart = [(2, 2), (2, 3), (3, 2), (2, 1), (1, 2), (3, 3), (1, 1), (3, 1), (1, 3), (0, 2), (2, 0), (0, 1), (1, 0), (0, 3), (3, 0)]
    peers = [4 * lax.rem(lax.div(me, 4) + y, 4) + lax.rem(lax.rem(me, 4) + x, 4) for y, x in apart]

    def copy(source, target, send, recv, device):
        return pltpu.make_async_remote_copy(
            src_ref=source,
            dst_ref=target,
            send_sem=send,
            recv_sem=recv,
            device_id={"group": device},
            device_id_type=pl.DeviceIdType.MESH,
        )

    class Exchange:
        def __init__(self, source, target, send, recv):
            self.source, self.target, self.send, self.recv = source, target, send, recv

        def start(self):
            for first in range(0, self.source.shape[1], PIECE):
                self.start_piece(first)

        def start_piece(self, first):
            size = min(PIECE, self.source.shape[1])
            here = pl.ds(first, size)
            for device in peers:
                copy(self.source.at[device, here], self.target.at[me, here], self.send, self.recv, device).start()
            self.target[me, first : first + size] = self.source[me, first : first + size]

        def all(self):
            most = pl.ds(0, others)
            return copy(self.source.at[most], self.target.at[most], self.send, self.recv, peers[0])

        def arrived(self):
            self.all().wait_recv()

        def sent(self):
            self.all().wait_send()

    def item(i):
        return Exchange(item_out.at[i], item_in.at[i], item_send.at[i], item_recv.at[i])

    pack = Exchange(bucket, received, pack_send.at[0], pack_recv.at[0])
    late_pack = Exchange(late_bucket, late_received, pack_send.at[1], pack_recv.at[1])
    up = [Exchange(up_out.at[r], up_in.at[r], up_send.at[r], up_recv.at[r]) for r in range(rounds)]
    down = [Exchange(down_out.at[r], down_in.at[r], down_send.at[r], down_recv.at[r]) for r in range(2 * rounds)]
    step_up = [item(r) for r in range(rounds)]
    step_down = [item(rounds + r) for r in range(rounds)]
    ask_up = [item(2 * rounds + r) for r in range(rounds)]
    ask_down = [item(3 * rounds + r) for r in range(rounds)]
    tail_up = item(4 * rounds)
    root_down = item(4 * rounds + 1)
    root_up = Exchange(root_out, root_in, root_send.at[0], root_recv.at[0])
    everything = [pack, late_pack, *up, *down, *step_up, *step_down, *ask_up, *ask_down, tail_up, root_down, root_up]

    barrier = pltpu.get_barrier_semaphore()
    for device in peers:
        pl.semaphore_signal(barrier, inc=1, device_id={"group": device}, device_id_type=pl.DeviceIdType.MESH)
    for fetch in fetches:
        fetch.start()

    def pair(level):
        both = jnp.concatenate([to_parent[0, level], grandparent[0, level]], axis=0)
        return product(halves(both), inverses[0, level])

    def ask(r, both):
        near[r] = halves(both)
        item_out[2 * rounds + r] = jnp.concatenate([both[:rows], both[rows:]], axis=1).reshape(blocks)

    fetches[0].wait()

    spread = lax.div(lax.broadcasted_iota(jnp.int32, (nodes, rows), 1), part)
    spread = spread == lax.broadcasted_iota(jnp.int32, (nodes, rows), 0)
    spread = jnp.where(spread, 1.0, 0.0).astype(jnp.bfloat16)
    names = parents[...].astype(jnp.float32).astype(jnp.bfloat16)
    over = (((0,), (1,)), ((), ()))
    across = mm(names, spread).astype(jnp.int32)
    along = lax.dot_general(spread, names, over, preferred_element_type=jnp.float32).astype(jnp.int32)
    place_r = lax.broadcasted_iota(jnp.int32, (rows, rows), 0)
    place_c = lax.broadcasted_iota(jnp.int32, (rows, rows), 1)
    same = lax.rem(place_r, part) == lax.rem(place_c, part)
    for l in range(levels - 1):
        hit = same & (lax.div(place_r, part) == across[l : l + 1, :])
        parent_map[l] = jnp.where(hit, 1.0, 0.0).astype(jnp.bfloat16)
        hit = same & (lax.div(place_c, part) == along[:, l : l + 1])
        child_map[l] = jnp.where(hit, 1.0, 0.0).astype(jnp.bfloat16)

    for fetch in fetches[1:4]:
        fetch.wait()
    ask(0, pair(1))
    ask(1, pair(3))
    last_step = product(halves(to_parent[0, levels - 2]), inverses[0, levels - 2])
    six[...] = halves(last_step)
    root_out[...] = last_step.reshape(nodes, part, rows)
    pl.semaphore_wait(barrier, others)
    ask_up[0].start()
    ask_up[1].start()
    root_up.start()
    for fetch in fetches[4:6]:
        fetch.wait()

    dof = jnp.concatenate([gluing[i : i + 1, :] for i in range(gluing.shape[0])], axis=1)
    sign = jnp.concatenate([signs[i : i + 1, :] for i in range(signs.shape[0])], axis=1)
    coeff = (2 * sign - 1).astype(jnp.float32)
    span = levels * rows
    node = lax.div(dof, span)
    row = lax.rem(dof, span)
    order = lax.broadcasted_iota(jnp.int32, (1, count), 1)
    key = (dof * count + order).astype(jnp.float32)
    first_key = (node * (span * count)).astype(jnp.float32)
    rank = jnp.zeros((1, count), jnp.float32)
    for i in range(count // 128):
        lanes = jnp.broadcast_to(key[:, i * 128 : (i + 1) * 128], (128, 128))
        down_key = jnp.transpose(lanes)
        down_key = jnp.concatenate([down_key] * (count // 128), axis=1)
        before = (down_key < key) & (down_key >= first_key)
        rank = rank + jnp.sum(jnp.where(before, 1.0, 0.0), axis=0, keepdims=True)
    place = rank.astype(jnp.int32) + 1
    fine = place < jnp.where(row < 2 * rows, EARLY, EARLY + LATE)
    overflow = jnp.max(jnp.where(fine, 0.0, 1.0))

    owned = lax.broadcasted_iota(jnp.int32, (nodes, count), 0) == node
    low_part = jnp.where(owned, lax.rem(row, rows).astype(jnp.float32), 0.0).astype(jnp.bfloat16)
    high_part = jnp.where(owned, (lax.div(row, rows) * rows).astype(jnp.float32), 0.0).astype(jnp.bfloat16)
    lane_of = lax.broadcasted_iota(jnp.int32, (columns, count), 0) == place
    lane_of = jnp.where(lane_of, 1.0, 0.0).astype(jnp.bfloat16)
    contract = (((1,), (1,)), ((), ()))
    header = lax.dot_general(low_part, lane_of, contract, preferred_element_type=jnp.float32)
    header = header + lax.dot_general(high_part, lane_of, contract, preferred_element_type=jnp.float32)
    lane = lax.broadcasted_iota(jnp.int32, header.shape, 1)
    header = jnp.where(lane == 0, -1.0, jnp.where(lane < EARLY + LATE, header, overflow))

    fetches[6].wait()
    m_high, m_low = split(multipliers[...])

    def packed(first, size):
        index = lax.broadcasted_iota(jnp.int32, (nodes * size, count), 0)
        inside = (place >= first) & (place < first + size)
        table = jnp.where(index == jnp.where(inside, node * size + place - first, -1), coeff, 0.0).astype(jnp.bfloat16)
        return (mm(table, m_high) + mm(table, m_low)).reshape(nodes, size, columns)

    bucket[...] = packed(0, EARLY)
    for n in range(nodes):
        bucket[n, 0:1, :] = header[n : n + 1, :]
    pack.start()
    late_bucket[...] = packed(EARLY, LATE)

    own[0] = pair(0)

    @pl.loop(0, levels)
    def _(l):
        inverse[l] = halves(inverses[0, l])

    def chain(a, b):
        return mm(a, b).astype(jnp.bfloat16)

    for r in range(rounds):
        w0, w1, w2 = parent_map[2 * r], parent_map[2 * r + 1], parent_map[2 * r + 2]
        near_map[r] = jnp.concatenate([w1, chain(w1, w0)], axis=1)
        both = chain(w2, w1)
        far_map[r] = jnp.concatenate([both, chain(both, w0), w2], axis=1)

    def gather(table, values):
        high, low = split(values)
        return mm(table, high) + mm(table, low)

    def answer(r):
        ask_up[r].arrived()
        found = gather(child_map[2 * r], item_in[2 * rounds + r].reshape(rows, columns))
        item_out[3 * rounds + r] = found.reshape(blocks)
        ask_down[r].start()

    def compose(r):
        ask_down[r].arrived()
        found = item_in[3 * rounds + r].reshape(rows, columns)
        found = jnp.concatenate([found[:, :rows], found[:, rows:]], axis=0)
        step = own[r, :rows]
        leap = own[r, rows:]
        made = product(halves(found), step)
        remote = -made[rows:]
        if r == rounds - 1:
            beyond = item_in[4 * rounds + 1].reshape(rows, columns)[:, rows:]
            remote = remote - product(halves(beyond), leap)
        far[r] = halves(jnp.concatenate([leap - made[:rows], remote, step], axis=0))

    answer(0)
    late_pack.start()

    width = nodes * EARLY

    def glue(level, wanted, source):
        table = lax.broadcasted_iota(jnp.int32, (rows, wanted.shape[1]), 0) + level * rows == wanted
        table = jnp.where(table, 1.0, 0.0).astype(jnp.bfloat16)
        return mm(table, source[0]) + mm(table, source[1])

    fetches[7].wait()
    pack.arrived()
    head = jnp.concatenate([received[n, 0:1, :] for n in range(nodes)], axis=0)
    flag[0, 0] = jnp.where(jnp.max(head[:, EARLY + LATE :]) > 0.0, 1, 0)

    def wide(first, size):
        lanes = lax.broadcasted_iota(jnp.int32, (columns, nodes * size), 1)
        pick = lax.rem(lanes, size) + first == lax.broadcasted_iota(jnp.int32, (columns, nodes * size), 0)
        pick = jnp.where(pick, 1.0, 0.0).astype(jnp.bfloat16)
        high, low = split(head)
        found = mm(high, pick) + mm(low, pick)
        sender = lax.div(lax.broadcasted_iota(jnp.int32, found.shape, 1), size)
        mine = sender == lax.broadcasted_iota(jnp.int32, found.shape, 0)
        return jnp.sum(jnp.where(mine, found, 0.0), axis=0, keepdims=True).astype(jnp.int32)

    early_rows = wide(0, EARLY)
    high, low = split(received[...].reshape(width, columns))
    rows_high[:width], rows_low[:width] = high, low
    for l in range(2):
        pending[l] = loads[0, l] - glue(l, early_rows, (high, low))

    def solve(level, x):
        out[0, level] = product(inverse[level], x)

    def skipped(r):
        step_down[r].arrived()
        solve(2 * r + 1, pending[2 * r + 1] - item_in[rounds + r].reshape(rows, columns))

    for r in range(rounds):
        level = 2 * r
        if r > 0:
            down[2 * r - 1].arrived()
            pending[level + 1] = pending[level + 1] - down_in[2 * r - 1].reshape(rows, columns)
        e = product(near[r], pending[level + 1])
        up_out[r, :, 0:part] = e[:rows].reshape(blocks)
        up_out[r, :, part : 2 * part] = e[rows:].reshape(blocks)
        up[r].start_piece(0)
        if r == 0:
            compose(0)
        else:
            down[2 * r - 2].arrived()
            pending[level] = pending[level] - down_in[2 * r - 2].reshape(rows, columns)
        c = product(far[r, : 2 * rows], pending[level])
        up_out[r, :, 2 * part : 3 * part] = c[:rows].reshape(blocks)
        up_out[r, :, 3 * part :] = c[rows:].reshape(blocks)
        up[r].start_piece(2 * part)
        item_out[r] = product(far[r, 2 * rows :], pending[level]).reshape(blocks)
        step_up[r].start()
        solve(level, pending[level])

        if r == 0:
            answer(1)
            step_five[...] = pair(5)
            for later in range(1, rounds):
                own[later] = pair(2 * later)
            late_pack.arrived()
            every_row = jnp.concatenate([early_rows, wide(EARLY, LATE)], axis=1)
            rows_high[width:], rows_low[width:] = split(late_received[...].reshape(nodes * LATE, columns))

            @pl.loop(2, levels)
            def _(l):
                pending[l] = loads[0, l] - glue(l, every_row, (rows_high[...], rows_low[...]))

            root_up.arrived()
            six_in = root_in[...].reshape(rows, rows)
            above = gather(child_map[5], six_in)
            above = jnp.concatenate([above, gather(child_map[4], above)], axis=1)
            item_out[4 * rounds + 1] = above.reshape(blocks)
            root_down.start()
            item_out[4 * rounds] = product(six[...], pending[levels - 2]).reshape(blocks)
        else:
            skipped(r - 1)
        if r == 1:
            answer(2)

        up[r].arrived()
        second = jnp.concatenate([up_in[r, :, i * part : (i + 1) * part].reshape(rows, columns) for i in (1, 3)], axis=0)
        if r == rounds - 1:
            tail_up.arrived()
            second = jnp.concatenate([second, item_in[4 * rounds].reshape(rows, columns)], axis=0)
            second = gather(far_map[r], second)
        else:
            second = gather(far_map[r, :, : 2 * rows], second)
        down_out[2 * r + 1] = second.reshape(blocks)
        down[2 * r + 1].start()
        first = jnp.concatenate([up_in[r, :, i * part : (i + 1) * part].reshape(rows, columns) for i in (0, 2)], axis=0)
        down_out[2 * r] = gather(near_map[r], first).reshape(blocks)
        down[2 * r].start()
        if r == 1:
            tail_up.start()
        step_up[r].arrived()
        item_out[rounds + r] = gather(parent_map[level], item_in[r].reshape(rows, columns)).reshape(blocks)
        step_down[r].start()

        if r == 0:
            root_down.arrived()
            beyond = item_in[4 * rounds + 1].reshape(rows, columns)[:, :rows]
            five = step_five[...]
            ask(2, jnp.concatenate([five[:rows], five[rows:] - product(halves(beyond), five[:rows])], axis=0))
            ask_up[2].start()
        if r < rounds - 1:
            compose(r + 1)

    down[2 * rounds - 1].arrived()
    solve(levels - 1, pending[levels - 1] - down_in[2 * rounds - 1].reshape(rows, columns))
    down[2 * rounds - 2].arrived()
    solve(levels - 2, pending[levels - 2] - down_in[2 * rounds - 2].reshape(rows, columns))
    skipped(rounds - 1)

    for exchange in everything:
        exchange.sent()


def direct(loads, multipliers, gluing, signs, parents, inverses, to_parent, grandparent_factor):
    nodes = parents.shape[0]
    _, levels, rows, columns = loads.shape
    count = multipliers.shape[0]
    f32, bf16 = jnp.float32, jnp.bfloat16
    rounds = levels // 2 - 1
    part = rows // nodes
    items = 4 * rounds + 2
    dma = pltpu.SemaphoreType.DMA
    vmem = pl.BlockSpec(memory_space=pltpu.VMEM)
    return pl.pallas_call(
        kernel,
        out_shape=(
            jax.ShapeDtypeStruct(loads.shape, f32),
            jax.ShapeDtypeStruct((1, 1), jnp.int32),
        ),
        in_specs=[pl.BlockSpec(memory_space=pltpu.HBM)] * 8,
        out_specs=(vmem, pl.BlockSpec(memory_space=pltpu.SMEM)),
        scratch_shapes=[
            pltpu.VMEM(loads.shape, f32),
            pltpu.VMEM(multipliers.shape, f32),
            pltpu.VMEM((count // 128, 128), jnp.int32),
            pltpu.VMEM((count // 128, 128), jnp.int32),
            pltpu.VMEM((levels - 1, nodes), jnp.int32),
            pltpu.VMEM(inverses.shape, f32),
            pltpu.VMEM(to_parent.shape, f32),
            pltpu.VMEM(grandparent_factor.shape, f32),
            dma((8,)),
            pltpu.VMEM((nodes, EARLY, columns), f32),
            pltpu.VMEM((nodes, EARLY, columns), f32),
            pltpu.VMEM((nodes, LATE, columns), f32),
            pltpu.VMEM((nodes, LATE, columns), f32),
            pltpu.VMEM((nodes * (EARLY + LATE), columns), bf16),
            pltpu.VMEM((nodes * (EARLY + LATE), columns), bf16),
            pltpu.VMEM((levels, rows, columns), f32),
            pltpu.VMEM((levels - 1, rows, rows), bf16),
            pltpu.VMEM((levels - 1, rows, rows), bf16),
            pltpu.VMEM((rounds, rows, 2 * rows), bf16),
            pltpu.VMEM((rounds, rows, 3 * rows), bf16),
            pltpu.VMEM((levels, rows, 2 * rows), bf16),
            pltpu.VMEM((rounds, 2 * rows, 2 * rows), bf16),
            pltpu.VMEM((rounds, 3 * rows, 2 * rows), bf16),
            pltpu.VMEM((rows, 2 * rows), bf16),
            pltpu.VMEM((2 * rows, rows), f32),
            pltpu.VMEM((rounds, 2 * rows, rows), f32),
            pltpu.VMEM((rounds, nodes, 4 * part, columns), f32),
            pltpu.VMEM((rounds, nodes, 4 * part, columns), f32),
            pltpu.VMEM((2 * rounds, nodes, part, columns), f32),
            pltpu.VMEM((2 * rounds, nodes, part, columns), f32),
            pltpu.VMEM((items, nodes, part, columns), f32),
            pltpu.VMEM((items, nodes, part, columns), f32),
            pltpu.VMEM((nodes, part, rows), f32),
            pltpu.VMEM((nodes, part, rows), f32),
            dma((2,)),
            dma((2,)),
            dma((rounds,)),
            dma((rounds,)),
            dma((2 * rounds,)),
            dma((2 * rounds,)),
            dma((items,)),
            dma((items,)),
            dma((1,)),
            dma((1,)),
        ],
        compiler_params=pltpu.CompilerParams(
            collective_id=0, has_side_effects=True, vmem_limit_bytes=48 * 1024 * 1024
        ),
    )(
        loads,
        multipliers,
        gluing.reshape(count // 128, 128),
        signs.reshape(count // 128, 128),
        parents.T,
        inverses,
        to_parent,
        grandparent_factor,
    )


def general(loads, multipliers, gluing, signs, parents, inverses, to_parent, grandparent_factor):
    me = lax.axis_index("group")
    size = lax.axis_size("group")
    levels, rows, columns = loads.shape[1:]
    span = levels * rows
    ring = [(i, (i + 1) % size) for i in range(size)]
    exact = lax.Precision.HIGHEST

    def passed(value):
        return lax.ppermute(value, "group", ring)

    target = (me * span + lax.iota(jnp.int32, span)).astype(jnp.float32)

    def add(_, state):
        glued, values, at = state
        table = jnp.where(target[:, None] == at[None, :], 1.0, 0.0)
        glued = glued + jnp.dot(table, values, precision=exact)
        return glued, passed(values), passed(at)

    coeff = (2 * signs - 1).astype(jnp.float32)
    start = (jnp.zeros((span, columns), jnp.float32), coeff[:, None] * multipliers, gluing.astype(jnp.float32))
    glued = lax.fori_loop(0, size, add, start)[0]
    pending = loads[0] - glued.reshape(levels, rows, columns)
    pending = jnp.concatenate([pending, jnp.zeros((2, rows, columns), jnp.float32)])
    one = jnp.concatenate([to_parent[0], jnp.zeros((1, rows, rows), jnp.float32)])
    two = jnp.concatenate([grandparent_factor[0], jnp.zeros((2, rows, rows), jnp.float32)])
    firsts = jnp.concatenate([parents, jnp.zeros((size, 2), jnp.int32)], axis=1)

    def level(l, state):
        pending, solved = state
        x = jnp.dot(inverses[0, l], pending[l], precision=exact)
        solved = solved.at[l].set(x)
        first = firsts[:, l]
        second = firsts[first, l + 1]

        def take(s, state):
            here, there, up, leap = state
            source = lax.rem(me - s + size, size)
            here = here + jnp.where(first[source] == me, up, 0.0)
            there = there + jnp.where(second[source] == me, leap, 0.0)
            return here, there, passed(up), passed(leap)

        zero = jnp.zeros((rows, columns), jnp.float32)
        up = jnp.dot(one[l], x, precision=exact)
        leap = jnp.dot(two[l], x, precision=exact)
        here, there, _, _ = lax.fori_loop(0, size, take, (zero, zero, up, leap))
        return pending.at[l + 1].add(-here).at[l + 2].add(-there), solved

    solved = lax.fori_loop(0, levels, level, (pending, jnp.zeros(loads.shape[1:], jnp.float32)))[1]
    return solved[None]


def finish_kernel(source, target, done):
    pieces = [pltpu.make_async_copy(source.at[0, l], target.at[0, l], done.at[l]) for l in range(source.shape[1])]
    for piece in pieces:
        piece.start()
    for piece in pieces:
        piece.wait()


def finish(solved):
    return pl.pallas_call(
        finish_kernel,
        out_shape=jax.ShapeDtypeStruct(solved.shape, solved.dtype),
        in_specs=[pl.BlockSpec(memory_space=pltpu.VMEM)],
        out_specs=pl.BlockSpec(memory_space=pl.ANY),
        scratch_shapes=[pltpu.SemaphoreType.DMA((solved.shape[1],))],
    )(solved)


def body(*args):
    solved, flag = direct(*args)
    return lax.switch(flag[0, 0], (lambda: finish(solved), lambda: general(*args)))


def solution(mesh):
    return jax.shard_map(
        body,
        mesh=mesh,
        in_specs=(
            P(("cluster", "group"), None, None, None),
            P(("cluster", "group"), None),
            P(("cluster", "group")),
            P(("cluster", "group")),
            P("cluster", None),
            P(("cluster", "group"), None, None, None),
            P(("cluster", "group"), None, None, None),
            P(("cluster", "group"), None, None, None),
        ),
        out_specs=P(("cluster", "group"), None, None, None),
        check_vma=False,
    )
```
